512 devices in a mesh: table: 32 (over x, z_lo, core), replica: 16 (over y, z_hi).
Axes of the slice: x: 4, y: 4, z: 16 (z_hi: 4, z_lo: 4; z = z_hi * 4 + z_lo), core: 2. Of those that a mesh axis runs over, the one named last changes fastest.
Arguments:
- top_input: bfloat16 [16384, 2048], P('replica'), may hold values from -6 to 6
- cotangent: bfloat16 [2048, 16384], P('table', 'replica'), may hold values from -0.25 to 0.25
- w_first: bfloat16 [2048, 2048], P('table'), may hold values from -0.125 to 0.125
- w_second: bfloat16 [2048, 2048], P('table'), may hold values from -0.125 to 0.125
- sectioned_rows: float32 [16, 128, 256, 256], P('replica', 'table'), may hold values from -6 to 6
- projection: bfloat16 [128, 256, 256], P('table'), may hold values from -0.375 to 0.375
- bag_ids: int32 [16, 256, 128, 16], P('replica', None, 'table'), may hold values from 0 to 255
- bag_lengths: int32 [16, 256, 128], P('replica', None, 'table'), may hold values from 1 to 16
- table_width: int32 [128], P('table'), may hold values from 32 to 256, as said below
Outputs:
- grad_first: bfloat16 [2048, 2048], P('table')
- grad_second: bfloat16 [2048, 2048], P('table')
- pooled_rows: bfloat16 [16, 256, 32768], P('replica', 'table')
The draws below stay inside these ranges and needn't reach their ends.
Inputs may be any that keep to these rules, and one draw needn't show every extreme that they name: `table_width`: each table's width is 256 // 8 times 1, 2, 4 or 8.
All inputs are finite; a program needn't handle non-finite values.
Results may differ from the reference program's by a relative error of at most 0.0051.
Values may be sent and summed in bfloat16 or wider, within the bound.
A program may use at most 64 MiB of HBM per device.

```python
import jax
import jax.numpy as jnp
from jax import lax

HID = 2048
EMB = 256
WMAX = 256
BAG = 16
ROWS = 256
TABLES = 128
SAMPLES = 256
GROUPS = 16
ROWS_ALL = 16384


def draw_table_width(key, part):
    key = jax.random.fold_in(key, 5)
    powers = jax.random.randint(key, (TABLES,), 0, 4)
    factors = jnp.array([1, 2, 4, 8], dtype=jnp.int32)
    return (WMAX // 8 * factors[powers]).astype(jnp.int32)


def plant(values, key, least, high):
    dims = values.shape
    spot = [jax.random.randint(jax.random.fold_in(key, axis), (), 0, dims[axis]) for axis in range(len(dims))]
    values = values.at[tuple(spot)].set(least)
    longest = dims.index(max(dims))
    spot[longest] = (spot[longest] + 1) % dims[longest]
    return values.at[tuple(spot)].set(high)


def level_of(rng, shape, pieces, low, largest):
    def one(axis_at, parts):
        steps = jax.random.uniform(jax.random.fold_in(jax.random.fold_in(rng, 6), axis_at), (parts,), jnp.float32, low / len(pieces), largest / len(pieces))
        return jnp.repeat(jnp.exp(steps), shape[axis_at] // parts).reshape((-1,) + (1,) * (len(shape) - axis_at - 1))

    factor_of = one(*pieces[0])
    for cut in pieces[1:]:
        factor_of = factor_of * one(*cut)
    return factor_of


def scatter_about(stream_key, extent, width, bound, shards=(), kind=jnp.bfloat16):
    loudness = level_of(stream_key, extent, shards, -0.22, 0.18) if shards else 1.0
    values = jax.random.normal(stream_key, extent, jnp.float32) * width * loudness
    return jnp.minimum(jnp.maximum(values, -bound), bound).astype(kind)


def setup_inputs(seed: int = 0) -> dict:
    key_of = jax.random.split(jax.random.key(seed), 10)
    return {
        "top_input": scatter_about(key_of[0], (ROWS_ALL, HID), 1.0, 6.0, ((0, 16),)),
        "cotangent": scatter_about(key_of[1], (HID, ROWS_ALL), 0.015625, 0.25, ((0, 32), (1, 16))),
        "w_first": scatter_about(key_of[2], (HID, HID), HID ** -0.5, 0.125, ((0, 32),)),
        "w_second": scatter_about(key_of[3], (HID, HID), HID ** -0.5, 0.125, ((0, 32),)),
        "sectioned_rows": scatter_about(key_of[4], (GROUPS, TABLES, ROWS, WMAX), 0.5, 6.0, ((0, 16), (1, 32)), jnp.float32),
        "projection": scatter_about(key_of[5], (TABLES, WMAX, EMB), WMAX ** -0.5, 0.375, ((0, 32),)),
        "bag_ids": plant(jax.random.randint(key_of[6], (GROUPS, SAMPLES, TABLES, BAG), 0, ROWS), jax.random.fold_in(key_of[6], 1), 0, ROWS - 1).astype(jnp.int32),
        "bag_lengths": plant(jax.random.randint(key_of[7], (GROUPS, SAMPLES, TABLES), 1, BAG + 1), jax.random.fold_in(key_of[7], 1), 1, BAG).astype(jnp.int32),
        "table_width": draw_table_width(jax.random.fold_in(key_of[9], 71), 0),
    }


def pool_table(operands):
    identities, lengths_here, sectioned_here, width_here, weight_here = operands
    bag_slots = jnp.arange(identities.shape[1], dtype=jnp.int32)
    present = bag_slots[None, :] < lengths_here[:, None]
    row_numbers = jnp.arange(sectioned_here.shape[0], dtype=jnp.int32)
    matches = jnp.logical_and(present[:, :, None], identities[:, :, None] == row_numbers[None, None, :])
    counts = jnp.sum(matches.astype(jnp.float32), axis=1)
    pooled = jnp.dot(counts, sectioned_here, precision=lax.Precision.HIGHEST, preferred_element_type=jnp.float32)
    columns = jnp.arange(sectioned_here.shape[1], dtype=jnp.int32)
    masked = jnp.where(columns[None, :] < width_here, pooled, jnp.zeros_like(pooled)).astype(jnp.bfloat16)
    return jnp.dot(masked, weight_here, preferred_element_type=jnp.float32).astype(jnp.bfloat16)


def reference(top_input, cotangent, w_first, w_second, sectioned_rows, projection, bag_ids, bag_lengths, table_width):
    pre_act = jnp.dot(top_input, w_first.T, preferred_element_type=jnp.float32)
    logistic = jax.nn.sigmoid(pre_act)
    hidden = (pre_act * logistic).astype(jnp.bfloat16)
    slopes = logistic * (1.0 + pre_act * (1.0 - logistic))
    d_output = cotangent.T
    grad_second = jnp.dot(hidden.T, d_output, preferred_element_type=jnp.float32).astype(jnp.bfloat16)
    d_hidden = jnp.dot(d_output, w_second.T, preferred_element_type=jnp.float32)
    d_pre = (d_hidden * slopes).astype(jnp.bfloat16)
    grad_first = jnp.dot(d_pre.T, top_input, preferred_element_type=jnp.float32).astype(jnp.bfloat16)

    def pool_group(operands):
        identities, lengths_here, sectioned_here = operands
        per_table = lax.map(pool_table, (jnp.transpose(identities, (1, 0, 2)), jnp.transpose(lengths_here), sectioned_here, table_width, projection))
        return jnp.transpose(per_table, (1, 0, 2)).reshape(per_table.shape[1], -1)

    pooled_rows = lax.map(pool_group, (bag_ids, bag_lengths, sectioned_rows))
    return grad_first, grad_second, pooled_rows
```

```python
import jax
import jax.numpy as jnp
from jax import lax
from jax.experimental import pallas as pl
from jax.experimental.pallas import tpu as pltpu
from jax.sharding import PartitionSpec as P

MESH = pl.DeviceIdType.MESH
F32 = jnp.float32
BF16 = jnp.bfloat16

HIDDEN = 64
ROWS = 1024
FEATS = 2048
BLOCK = 64
PIECE = 512
PIECES = 4
SHARE = 16
PEERS = 32
TABLES = 4
LANES = 256

Z_AT = 0
X_AT = Z_AT + 3
HALF_AT = X_AT + 8
CORE_AT = HALF_AT + 8
PIECE_AT = CORE_AT + 16
SPREAD_AT = PIECE_AT + 9 * 2 * PIECES
COPIES = SPREAD_AT + PEERS - 1


def wrap(value, size):
    return lax.rem(value + size, size)


def kernel(
    widths,
    top_hbm,
    cot_hbm,
    first_hbm,
    second_hbm,
    rows_hbm,
    proj_hbm,
    ids_hbm,
    lens_hbm,
    out_first,
    out_second,
    out_pooled,
    top,
    cot,
    first,
    second,
    rows,
    proj,
    ids,
    lens,
    hidden,
    slope,
    d_hidden,
    part,
    part_b,
    y_in,
    z_in,
    result,
    spread,
    arrived,
    local_sem,
    send_sem,
    recv_sem,
):
    table = lax.axis_index("table")
    replica = lax.axis_index("replica")
    x = lax.div(table, 8)
    z = lax.rem(lax.div(table, 2), 4)
    c = lax.rem(table, 2)
    y = lax.div(replica, 4)
    zh = lax.rem(replica, 4)

    def table_of(x_, z_, c_):
        return x_ * 8 + z_ * 2 + c_

    def block(x_, z_, c_, half=None):
        start = table_of(x_, z_, c_) * BLOCK
        if half is None:
            return cot.at[pl.ds(pl.multiple_of(start, BLOCK), BLOCK)]
        size = BLOCK // 2
        return cot.at[pl.ds(pl.multiple_of(start + half * size, size), size)]

    def remote(number, src, dst, to_table, to_replica):
        return pltpu.make_async_remote_copy(
            src_ref=src,
            dst_ref=dst,
            send_sem=send_sem.at[number],
            recv_sem=recv_sem.at[number],
            device_id=(to_table, to_replica),
            device_id_type=MESH,
        )

    sent = []

    def send(number, src, dst, to_table, to_replica):
        copy = remote(number, src, dst, to_table, to_replica)
        copy.start()
        sent.append(copy)

    def receive(number, dst):
        remote(number, dst, dst, table, replica).wait_recv()

    def local(number, src, dst):
        copy = pltpu.make_async_copy(src, dst, local_sem.at[number])
        copy.start()
        return copy

    mine = block(x, z, c)
    load_cot = local(0, cot_hbm, mine)
    load_first = local(1, first_hbm, first)
    load_top = local(2, top_hbm, top)
    load_ids = local(3, ids_hbm, ids)
    load_lens = local(4, lens_hbm, lens)
    load_rows = local(5, rows_hbm, rows)
    load_proj = local(6, proj_hbm, proj)
    load_second = local(7, second_hbm, second)

    barrier = pltpu.get_barrier_semaphore()
    for k in range(1, PEERS):
        pl.semaphore_signal(
            barrier, inc=1, device_id=(wrap(table + k, PEERS), replica), device_id_type=MESH
        )
    for k in range(1, 4):
        pl.semaphore_signal(
            barrier, inc=1, device_id=(table, wrap(y + k, 4) * 4 + zh), device_id_type=MESH
        )
        pl.semaphore_signal(
            barrier, inc=1, device_id=(table, y * 4 + wrap(zh + k, 4)), device_id_type=MESH
        )
    load_cot.wait()
    pl.semaphore_wait(barrier, PEERS - 1 + 6)

    x_up, x_down, x_far = wrap(x + 1, 4), wrap(x - 1, 4), wrap(x + 2, 4)
    columns = (x, x_up, x_down, x_far)

    def to_core(which, j):
        ref = block(columns[which], wrap(z + j, 4), c)
        send(CORE_AT + which * 4 + j, ref, ref, table_of(x, z, 1 - c), replica)

    def from_core(which):
        for j in range(4):
            ref = block(columns[which], wrap(z + j, 4), 1 - c)
            receive(CORE_AT + which * 4 + j, ref)

    def to_x(j):
        ref = block(x, wrap(z + j, 4), c)
        send(X_AT + j, ref, ref, table_of(x_up, z, c), replica)
        send(X_AT + 4 + j, ref, ref, table_of(x_down, z, c), replica)

    def from_x(j):
        zj = wrap(z + j, 4)
        receive(X_AT + j, block(x_down, zj, c))
        ref = block(x_down, zj, c, 0)
        send(HALF_AT + j, ref, ref, table_of(x_up, z, c), replica)
        receive(X_AT + 4 + j, block(x_up, zj, c))
        ref = block(x_up, zj, c, 1)
        send(HALF_AT + 4 + j, ref, ref, table_of(x_down, z, c), replica)
        to_core(2, j)
        to_core(1, j)

    def from_far(j):
        zj = wrap(z + j, 4)
        receive(HALF_AT + j, block(x_far, zj, c, 0))
        receive(HALF_AT + 4 + j, block(x_far, zj, c, 1))
        to_core(3, j)

    for k in (1, 3, 2):
        send(Z_AT + k - 1, mine, mine, table_of(x, wrap(z + k, 4), c), replica)
    to_x(0)
    to_core(0, 0)

    load_first.wait()
    load_top.wait()

    def forward(step, carry):
        at = pl.ds(pl.multiple_of(step * 256, 256), 256)
        pre = lax.dot_general(
            first[...], top[at, :], (((1,), (1,)), ((), ())), preferred_element_type=F32
        )
        s = 1.0 / (1.0 + jnp.exp(-pre))
        hidden[:, at] = (pre * s).astype(BF16)
        slope[:, at] = s * (1.0 + pre * (1.0 - s))
        return carry

    lax.fori_loop(0, 4, forward, 0)

    load_ids.wait()
    load_lens.wait()
    load_rows.wait()
    load_proj.wait()

    def pool(t):
        slots = lax.broadcasted_iota(jnp.int32, (16, LANES), 0)
        live = jnp.where(slots < lens[t : t + 1, :], ids[t], -1)
        numbers = lax.broadcasted_iota(jnp.int32, (LANES, LANES), 0)
        counts = jnp.zeros((LANES, LANES), F32)
        for k in range(16):
            counts = counts + jnp.where(live[k : k + 1, :] == numbers, 1.0, 0.0)
        counts = counts.T.astype(BF16)
        whole = rows[t]
        high = whole.astype(BF16)
        rest = whole - high.astype(F32)
        middle = rest.astype(BF16)
        low = (rest - middle.astype(F32)).astype(BF16)
        pooled = jnp.dot(counts, low, preferred_element_type=F32)
        pooled = pooled + jnp.dot(counts, middle, preferred_element_type=F32)
        pooled = pooled + jnp.dot(counts, high, preferred_element_type=F32)
        lanes = lax.broadcasted_iota(jnp.int32, (LANES, LANES), 1)
        kept = jnp.where(lanes < widths[t], pooled, 0.0).astype(BF16)
        return jnp.dot(kept, proj[t], preferred_element_type=F32)

    def pool_pair(t):
        upper = pool(t).reshape(PEERS, 8, LANES)
        lower = pool(t + 2).reshape(PEERS, 8, LANES)
        spread[:, :, t * LANES : (t + 1) * LANES] = jnp.concatenate([upper, lower], 1).astype(BF16)

    def column_step(which):
        at = pl.ds(pl.multiple_of(columns[which] * PIECE, PIECE), PIECE)
        there = cot[at, :]
        product = jnp.dot(second[:, at], there, preferred_element_type=F32)
        if which == 0:
            d_hidden[...] = product
        else:
            d_hidden[...] += product
        share_out(
            which,
            lax.dot_general(
                hidden[...], there, (((1,), (1,)), ((), ())), preferred_element_type=F32
            ),
        )

    def piece_at(p):
        if p < PIECES:
            return 1, pl.ds(pl.multiple_of(columns[p] * PIECE, PIECE), PIECE)
        return 0, pl.ds((p - PIECES) * PIECE, PIECE)

    def share(y_):
        return pl.ds(pl.multiple_of(y_ * SHARE, SHARE), SHARE)

    def share_out(p, value):
        part[p] = value
        part_b[p] = value.astype(BF16)
        for k in range(1, 4):
            to = wrap(y + k, 4)
            send(PIECE_AT + 9 * p + k - 1, part_b.at[p, share(to)], y_in.at[p, k - 1], table, to * 4 + zh)

    def exchange(p):
        total = part[p, share(y), :]
        for k in range(1, 4):
            receive(PIECE_AT + 9 * p + k - 1, y_in.at[p, k - 1])
            total = total + y_in[p, k - 1].astype(F32)
        z_in[p, zh] = total.astype(BF16)
        for k in range(1, 4):
            send(
                PIECE_AT + 9 * p + 3 + k - 1,
                z_in.at[p, zh],
                z_in.at[p, zh],
                table,
                y * 4 + wrap(zh + k, 4),
            )

    def finish(p):
        for k in (1, 3, 2):
            receive(PIECE_AT + 9 * p + 3 + k - 1, z_in.at[p, wrap(zh - k, 4)])
        total = z_in[p, 0].astype(F32)
        for k in range(1, 4):
            total = total + z_in[p, k].astype(F32)
        which, at = piece_at(p)
        result[which, share(y), at] = total.astype(BF16)
        ref = result.at[which, share(y), at]
        for k in range(1, 4):
            send(PIECE_AT + 9 * p + 6 + k - 1, ref, ref, table, wrap(y + k, 4) * 4 + zh)

    def collect(p):
        which, at = piece_at(p)
        for k in range(1, 4):
            receive(PIECE_AT + 9 * p + 6 + k - 1, result.at[which, share(wrap(y - k, 4)), at])

    from_x(0)
    pool_pair(0)
    for k in (1, 3, 2):
        receive(Z_AT + k - 1, block(x, wrap(z - k, 4), c))
        to_x(4 - k)
        to_core(0, 4 - k)
    pool_pair(1)
    load_second.wait()
    from_core(0)
    column_step(0)
    for j in (3, 1, 2):
        from_x(j)
    for k in range(1, PEERS):
        to = wrap(table + k, PEERS)
        send(SPREAD_AT + k - 1, spread.at[to], arrived.at[table], to, replica)
    arrived[table] = spread[table]
    exchange(0)
    from_core(1)
    column_step(1)
    from_core(2)
    column_step(2)
    for j in (0, 3, 1, 2):
        from_far(j)
    exchange(1)
    exchange(2)
    from_core(3)
    column_step(3)
    d_pre = (d_hidden[...] * slope[...]).astype(BF16)
    for q in range(PIECES):
        share_out(
            PIECES + q,
            jnp.dot(d_pre, top[:, q * PIECE : (q + 1) * PIECE], preferred_element_type=F32),
        )
    for p in range(3, 2 * PIECES):
        exchange(p)
    for p in range(2 * PIECES):
        finish(p)
    for k in range(1, PEERS):
        receive(SPREAD_AT + k - 1, arrived.at[wrap(table - k, PEERS)])

    def place(j, carry):
        value = arrived[j].astype(F32)
        start = pl.multiple_of(j * 1024, 1024)
        out_pooled[0, :, pl.ds(start, 512)] = value[:8].astype(BF16)
        out_pooled[0, :, pl.ds(start + 512, 512)] = value[8:].astype(BF16)
        return carry

    lax.fori_loop(0, PEERS, place, 0)
    for p in range(2 * PIECES):
        collect(p)
    out_first[...] = result[0]
    out_second[...] = result[1]
    for copy in sent:
        copy.wait_send()


def shards(
    top_input,
    cotangent,
    w_first,
    w_second,
    sectioned_rows,
    projection,
    bag_ids,
    bag_lengths,
    table_width,
):
    hbm = pl.BlockSpec(memory_space=pltpu.HBM)
    vmem = pl.BlockSpec(memory_space=pltpu.VMEM)
    ids = jnp.transpose(bag_ids[0], (1, 2, 0))
    lens = jnp.transpose(bag_lengths[0], (1, 0))
    return pl.pallas_call(
        kernel,
        out_shape=(
            jax.ShapeDtypeStruct((HIDDEN, FEATS), BF16),
            jax.ShapeDtypeStruct((HIDDEN, FEATS), BF16),
            jax.ShapeDtypeStruct((1, 8, PEERS * 1024), BF16),
        ),
        in_specs=[pl.BlockSpec(memory_space=pltpu.SMEM)] + [hbm] * 8,
        out_specs=(vmem, vmem, vmem),
        scratch_shapes=[
            pltpu.VMEM((ROWS, FEATS), BF16),
            pltpu.VMEM((FEATS, ROWS), BF16),
            pltpu.VMEM((HIDDEN, FEATS), BF16),
            pltpu.VMEM((HIDDEN, FEATS), BF16),
            pltpu.VMEM((TABLES, LANES, LANES), F32),
            pltpu.VMEM((TABLES, LANES, LANES), BF16),
            pltpu.VMEM((TABLES, 16, LANES), jnp.int32),
            pltpu.VMEM((TABLES, LANES), jnp.int32),
            pltpu.VMEM((HIDDEN, ROWS), BF16),
            pltpu.VMEM((HIDDEN, ROWS), F32),
            pltpu.VMEM((HIDDEN, ROWS), F32),
            pltpu.VMEM((2 * PIECES, HIDDEN, PIECE), F32),
            pltpu.VMEM((2 * PIECES, HIDDEN, PIECE), BF16),
            pltpu.VMEM((2 * PIECES, 3, SHARE, PIECE), BF16),
            pltpu.VMEM((2 * PIECES, 4, SHARE, PIECE), BF16),
            pltpu.VMEM((2, HIDDEN, FEATS), BF16),
            pltpu.VMEM((PEERS, 16, 512), BF16),
            pltpu.VMEM((PEERS, 16, 512), BF16),
            pltpu.SemaphoreType.DMA((8,)),
            pltpu.SemaphoreType.DMA((COPIES,)),
            pltpu.SemaphoreType.DMA((COPIES,)),
        ],
        compiler_params=pltpu.CompilerParams(
            collective_id=0, has_side_effects=True, vmem_limit_bytes=40 * 2**20
        ),
        cost_estimate=pl.CostEstimate(
            flops=2 * 4 * HIDDEN * ROWS * FEATS, bytes_accessed=8 * 2**20, transcendentals=HIDDEN * ROWS
        ),
    )(
        table_width,
        top_input,
        cotangent,
        w_first,
        w_second,
        sectioned_rows[0],
        projection,
        ids,
        lens,
    )


def solution(mesh):
    placed = (
        P("replica", None),
        P("table", "replica"),
        P("table", None),
        P("table", None),
        P("replica", "table", None, None),
        P("table", None, None),
        P("replica", None, "table", None),
        P("replica", None, "table"),
        P("table"),
    )
    return jax.shard_map(
        shards,
        mesh=mesh,
        in_specs=placed,
        out_specs=(P("table", None), P("table", None), P("replica", "table", None)),
        check_vma=False,
    )
```

```python
import jax
import jax.numpy as jnp
from jax import lax
from jax.experimental import pallas as pl
from jax.experimental.pallas import tpu as pltpu
from jax.sharding import PartitionSpec as P

MESH = pl.DeviceIdType.MESH
F32 = jnp.float32
BF16 = jnp.bfloat16

HIDDEN = 64
ROWS = 1024
FEATS = 2048
BLOCK = 64
PIECE = 512
PIECES = 4
SHARE = 16
PEERS = 32
TABLES = 4
LANES = 256

Z_AT = 0
X_AT = Z_AT + 3
HALF_AT = X_AT + 8
CORE_AT = HALF_AT + 8
PIECE_AT = CORE_AT + 16
SPREAD_AT = PIECE_AT + 9 * 2 * PIECES
COPIES = SPREAD_AT + 7 + 3


def wrap(value, size):
    return lax.rem(value + size, size)


def kernel(
    widths_hbm,
    top_hbm,
    cot_hbm,
    first_hbm,
    second_hbm,
    rows_hbm,
    proj_hbm,
    ids_hbm,
    lens_hbm,
    out_first,
    out_second,
    out_pooled,
    top,
    cot,
    first,
    second,
    rows,
    proj,
    ids,
    lens,
    widths,
    hidden,
    slope,
    d_hidden,
    part,
    part_b,
    y_in,
    z_in,
    result,
    spread,
    passing,
    arrived,
    local_sem,
    send_sem,
    recv_sem,
):
    table = lax.axis_index("table")
    replica = lax.axis_index("replica")
    x = lax.div(table, 8)
    z = lax.rem(lax.div(table, 2), 4)
    c = lax.rem(table, 2)
    y = lax.div(replica, 4)
    zh = lax.rem(replica, 4)

    def table_of(x_, z_, c_):
        return x_ * 8 + z_ * 2 + c_

    def block(x_, z_, c_, half=None):
        start = table_of(x_, z_, c_) * BLOCK
        if half is None:
            return cot.at[pl.ds(pl.multiple_of(start, BLOCK), BLOCK)]
        size = BLOCK // 2
        return cot.at[pl.ds(pl.multiple_of(start + half * size, size), size)]

    def remote(number, src, dst, to_table, to_replica):
        return pltpu.make_async_remote_copy(
            src_ref=src,
            dst_ref=dst,
            send_sem=send_sem.at[number],
            recv_sem=recv_sem.at[number],
            device_id=(to_table, to_replica),
            device_id_type=MESH,
        )

    sent = []

    def send(number, src, dst, to_table, to_replica):
        copy = remote(number, src, dst, to_table, to_replica)
        copy.start()
        sent.append(copy)

    def receive(number, dst):
        remote(number, dst, dst, table, replica).wait_recv()

    def local(number, src, dst):
        copy = pltpu.make_async_copy(src, dst, local_sem.at[number])
        copy.start()
        return copy

    mine = block(x, z, c)
    run = z * 2 + c
    load_cot = local(0, cot_hbm, mine)

    barrier = pltpu.get_barrier_semaphore()

    def greet(to_table, to_replica):
        pl.semaphore_signal(
            barrier, inc=1, device_id=(to_table, to_replica), device_id_type=MESH
        )

    for k in range(1, 8):
        greet(x * 8 + wrap(run + k, 8), replica)
    for k in range(1, 4):
        greet(wrap(x + k, 4) * 8 + run, replica)
    for k in range(1, 4):
        greet(table, wrap(y + k, 4) * 4 + zh)
        greet(table, y * 4 + wrap(zh + k, 4))
    load_first = local(1, first_hbm, first)
    load_top = local(2, top_hbm, top)
    load_ids = local(3, ids_hbm, ids)
    load_lens = local(4, lens_hbm, lens)
    load_rows = local(5, rows_hbm, rows)
    load_proj = local(6, proj_hbm, proj)
    load_second = local(7, second_hbm, second)
    load_widths = local(8, widths_hbm, widths)
    load_cot.wait()
    pl.semaphore_wait(barrier, 16)

    run_z = (z, z + 1 - 2 * lax.rem(z, 2), wrap(z + 2, 4), 3 - z)
    x_up, x_down, x_far = wrap(x + 1, 4), wrap(x - 1, 4), wrap(x + 2, 4)
    columns = (x, x_up, x_down, x_far)

    def to_core(which, j):
        ref = block(columns[which], run_z[j], c)
        send(CORE_AT + which * 4 + j, ref, ref, table_of(x, z, 1 - c), replica)

    def from_core(which):
        for j in range(4):
            ref = block(columns[which], run_z[j], 1 - c)
            receive(CORE_AT + which * 4 + j, ref)

    def to_x(j):
        ref = block(x, run_z[j], c)
        send(X_AT + j, ref, ref, table_of(x_up, z, c), replica)
        send(X_AT + 4 + j, ref, ref, table_of(x_down, z, c), replica)

    def from_x(j):
        zj = run_z[j]
        receive(X_AT + j, block(x_down, zj, c))
        ref = block(x_down, zj, c, 0)
        send(HALF_AT + j, ref, ref, table_of(x_up, z, c), replica)
        receive(X_AT + 4 + j, block(x_up, zj, c))
        ref = block(x_up, zj, c, 1)
        send(HALF_AT + 4 + j, ref, ref, table_of(x_down, z, c), replica)
        to_core(2, j)
        to_core(1, j)

    def from_far(j):
        zj = run_z[j]
        receive(HALF_AT + j, block(x_far, zj, c, 0))
        receive(HALF_AT + 4 + j, block(x_far, zj, c, 1))
        to_core(3, j)

    send(Z_AT, mine, mine, table_of(x, run_z[1], c), replica)
    to_x(0)
    for v in (3, 2):
        send(Z_AT + v - 1, mine, mine, table_of(x, run_z[v], c), replica)
    to_core(0, 0)

    load_first.wait()
    load_top.wait()

    def forward(step, carry):
        at = pl.ds(pl.multiple_of(step * 256, 256), 256)
        pre = lax.dot_general(
            first[...], top[at, :], (((1,), (1,)), ((), ())), preferred_element_type=F32
        )
        s = 1.0 / (1.0 + jnp.exp(-pre))
        hidden[:, at] = (pre * s).astype(BF16)
        slope[:, at] = s * (1.0 + pre * (1.0 - s))
        return carry

    lax.fori_loop(0, 4, forward, 0)

    load_ids.wait()
    load_lens.wait()
    load_rows.wait()
    load_proj.wait()
    load_widths.wait()

    def pool(t):
        slots = lax.broadcasted_iota(jnp.int32, (16, LANES), 0)
        live = jnp.where(slots < lens[t : t + 1, :], ids[t], -1)
        numbers = lax.broadcasted_iota(jnp.int32, (LANES, LANES), 0)
        counts = jnp.zeros((LANES, LANES), F32)
        for k in range(16):
            counts = counts + jnp.where(live[k : k + 1, :] == numbers, 1.0, 0.0)
        counts = counts.T.astype(BF16)
        whole = rows[t]
        high = whole.astype(BF16)
        rest = whole - high.astype(F32)
        middle = rest.astype(BF16)
        low = (rest - middle.astype(F32)).astype(BF16)
        pooled = jnp.dot(counts, low, preferred_element_type=F32)
        pooled = pooled + jnp.dot(counts, middle, preferred_element_type=F32)
        pooled = pooled + jnp.dot(counts, high, preferred_element_type=F32)
        lanes = lax.broadcasted_iota(jnp.int32, (LANES, LANES), 1)
        kept = jnp.where(lanes < widths[t], pooled, 0.0).astype(BF16)
        return jnp.dot(kept, proj[t], preferred_element_type=F32)

    def pool_pair(t):
        upper = pool(t).reshape(PEERS, 8, LANES)
        lower = pool(t + 2).reshape(PEERS, 8, LANES)
        both = jnp.concatenate([upper, lower], 1).astype(BF16)
        for to in range(4):
            spread[:, to, :, t * LANES : (t + 1) * LANES] = both[to * 8 : (to + 1) * 8]

    def column_step(which):
        at = pl.ds(pl.multiple_of(columns[which] * PIECE, PIECE), PIECE)
        there = cot[at, :]
        product = jnp.dot(second[:, at], there, preferred_element_type=F32)
        if which == 0:
            d_hidden[...] = product
        else:
            d_hidden[...] += product
        share_out(
            which,
            lax.dot_general(
                hidden[...], there, (((1,), (1,)), ((), ())), preferred_element_type=F32
            ),
        )

    def piece_at(p):
        if p < PIECES:
            return 1, pl.ds(pl.multiple_of(columns[p] * PIECE, PIECE), PIECE)
        return 0, pl.ds((p - PIECES) * PIECE, PIECE)

    def share(y_):
        return pl.ds(pl.multiple_of(y_ * SHARE, SHARE), SHARE)

    def share_out(p, value):
        part[p] = value
        part_b[p] = value.astype(BF16)
        for k in range(1, 4):
            to = wrap(y + k, 4)
            send(PIECE_AT + 9 * p + k - 1, part_b.at[p, share(to)], y_in.at[p, k - 1], table, to * 4 + zh)

    def exchange(p):
        total = part[p, share(y), :]
        for k in range(1, 4):
            receive(PIECE_AT + 9 * p + k - 1, y_in.at[p, k - 1])
            total = total + y_in[p, k - 1].astype(F32)
        z_in[p, zh] = total.astype(BF16)
        for k in range(1, 4):
            send(
                PIECE_AT + 9 * p + 3 + k - 1,
                z_in.at[p, zh],
                z_in.at[p, zh],
                table,
                y * 4 + wrap(zh + k, 4),
            )

    def finish(p):
        for k in (1, 3, 2):
            receive(PIECE_AT + 9 * p + 3 + k - 1, z_in.at[p, wrap(zh - k, 4)])
        total = z_in[p, 0].astype(F32)
        for k in range(1, 4):
            total = total + z_in[p, k].astype(F32)
        which, at = piece_at(p)
        result[which, share(y), at] = total.astype(BF16)
        ref = result.at[which, share(y), at]
        for k in range(1, 4):
            send(PIECE_AT + 9 * p + 6 + k - 1, ref, ref, table, wrap(y + k, 4) * 4 + zh)

    def collect(p):
        which, at = piece_at(p)
        for k in range(1, 4):
            receive(PIECE_AT + 9 * p + 6 + k - 1, result.at[which, share(wrap(y - k, 4)), at])

    def spread_run():
        for k in range(1, 8):
            to = wrap(run + k, 8)
            send(SPREAD_AT + k - 1, spread.at[to], passing.at[:, run], x * 8 + to, replica)
        passing[:, run] = spread[run]

    def spread_x():
        for k in range(1, 8):
            receive(SPREAD_AT + k - 1, passing.at[:, wrap(run - k, 8)])
        for k in (1, 3, 2):
            to = wrap(x + k, 4)
            send(SPREAD_AT + 7 + k - 1, passing.at[to], arrived.at[x], to * 8 + run, replica)
        arrived[x] = passing[x]

    def place_pooled():
        for k in (1, 3, 2):
            receive(SPREAD_AT + 7 + k - 1, arrived.at[wrap(x - k, 4)])

        def place(j, carry):
            value = arrived[lax.div(j, 8), lax.rem(j, 8)].astype(F32)
            start = pl.multiple_of(j * 1024, 1024)
            out_pooled[0, :, pl.ds(start, 512)] = value[:8].astype(BF16)
            out_pooled[0, :, pl.ds(start + 512, 512)] = value[8:].astype(BF16)
            return carry

        lax.fori_loop(0, PEERS, place, 0)

    pool_pair(0)
    pool_pair(1)
    from_x(0)
    for v in (1, 3, 2):
        receive(Z_AT + v - 1, block(x, run_z[v], c))
        to_x(v)
        to_core(0, v)
    spread_run()
    load_second.wait()
    from_core(0)
    column_step(0)
    for j in (1, 3, 2):
        from_x(j)
    exchange(0)
    from_core(1)
    column_step(1)
    from_core(2)
    column_step(2)
    for j in (0, 1, 3, 2):
        from_far(j)
    exchange(1)
    exchange(2)
    from_core(3)
    column_step(3)
    d_pre = (d_hidden[...] * slope[...]).astype(BF16)
    for q in range(PIECES):
        share_out(
            PIECES + q,
            jnp.dot(d_pre, top[:, q * PIECE : (q + 1) * PIECE], preferred_element_type=F32),
        )
    spread_x()
    for p in range(3, 2 * PIECES):
        exchange(p)
    finish(0)
    finish(1)
    finish(2)
    place_pooled()
    for copy in sent:
        copy.wait_send()
    sent.clear()
    for p in range(3, 2 * PIECES):
        finish(p)
    for p in range(2 * PIECES):
        collect(p)
    out_first[...] = result[0]
    out_second[...] = result[1]
    for copy in sent:
        copy.wait_send()


def shards(
    top_input,
    cotangent,
    w_first,
    w_second,
    sectioned_rows,
    projection,
    bag_ids,
    bag_lengths,
    table_width,
):
    hbm = pl.BlockSpec(memory_space=pltpu.HBM)
    vmem = pl.BlockSpec(memory_space=pltpu.VMEM)
    ids = jnp.transpose(bag_ids[0], (1, 2, 0))
    lens = jnp.transpose(bag_lengths[0], (1, 0))
    return pl.pallas_call(
        kernel,
        out_shape=(
            jax.ShapeDtypeStruct((HIDDEN, FEATS), BF16),
            jax.ShapeDtypeStruct((HIDDEN, FEATS), BF16),
            jax.ShapeDtypeStruct((1, 8, PEERS * 1024), BF16),
        ),
        in_specs=[hbm] * 9,
        out_specs=(vmem, vmem, vmem),
        scratch_shapes=[
            pltpu.VMEM((ROWS, FEATS), BF16),
            pltpu.VMEM((FEATS, ROWS), BF16),
            pltpu.VMEM((HIDDEN, FEATS), BF16),
            pltpu.VMEM((HIDDEN, FEATS), BF16),
            pltpu.VMEM((TABLES, LANES, LANES), F32),
            pltpu.VMEM((TABLES, LANES, LANES), BF16),
            pltpu.VMEM((TABLES, 16, LANES), jnp.int32),
            pltpu.VMEM((TABLES, LANES), jnp.int32),
            pltpu.SMEM((TABLES,), jnp.int32),
            pltpu.VMEM((HIDDEN, ROWS), BF16),
            pltpu.VMEM((HIDDEN, ROWS), F32),
            pltpu.VMEM((HIDDEN, ROWS), F32),
            pltpu.VMEM((2 * PIECES, HIDDEN, PIECE), F32),
            pltpu.VMEM((2 * PIECES, HIDDEN, PIECE), BF16),
            pltpu.VMEM((2 * PIECES, 3, SHARE, PIECE), BF16),
            pltpu.VMEM((2 * PIECES, 4, SHARE, PIECE), BF16),
            pltpu.VMEM((2, HIDDEN, FEATS), BF16),
            pltpu.VMEM((8, 4, 16, 512), BF16),
            pltpu.VMEM((4, 8, 16, 512), BF16),
            pltpu.VMEM((4, 8, 16, 512), BF16),
            pltpu.SemaphoreType.DMA((9,)),
            pltpu.SemaphoreType.DMA((COPIES,)),
            pltpu.SemaphoreType.DMA((COPIES,)),
        ],
        compiler_params=pltpu.CompilerParams(
            collective_id=0, has_side_effects=True, vmem_limit_bytes=40 * 2**20
        ),
        cost_estimate=pl.CostEstimate(
            flops=2 * 4 * HIDDEN * ROWS * FEATS, bytes_accessed=8 * 2**20, transcendentals=HIDDEN * ROWS
        ),
    )(
        *(
            pltpu.with_memory_space_constraint(value, pltpu.HBM)
            for value in (
                table_width,
                top_input,
                cotangent,
                w_first,
                w_second,
                sectioned_rows[0],
                projection,
                ids,
                lens,
            )
        )
    )


def solution(mesh):
    placed = (
        P("replica", None),
        P("table", "replica"),
        P("table", None),
        P("table", None),
        P("replica", "table", None, None),
        P("table", None, None),
        P("replica", None, "table", None),
        P("replica", None, "table"),
        P("table"),
    )
    return jax.shard_map(
        shards,
        mesh=mesh,
        in_specs=placed,
        out_specs=(P("table", None), P("table", None), P("replica", "table", None)),
        check_vma=False,
    )
```

```python
import jax
import jax.numpy as jnp
from jax import lax
from jax.experimental import pallas as pl
from jax.experimental.pallas import tpu as pltpu
from jax.sharding import PartitionSpec as P

MESH = pl.DeviceIdType.MESH
F32 = jnp.float32
BF16 = jnp.bfloat16

HIDDEN = 64
ROWS = 1024
FEATS = 2048
BLOCK = 64
RUN = 512
LINE = 256
CHUNKS = 4
CHUNK = ROWS // CHUNKS
PIECES = 4
PIECE = FEATS // PIECES
SHARE = 16
PEERS = 32
TABLES = 4
LANES = 256

Z_AT = 0
CORE_AT = Z_AT + 3 * CHUNKS
PARTIAL_AT = CORE_AT + 1 + 3 * CHUNKS
WEIGHT_AT = PARTIAL_AT + 3 * CHUNKS
HIDDEN_AT = WEIGHT_AT + 3
FIRST_AT = HIDDEN_AT + 3
SECOND_AT = FIRST_AT + 8 * PIECES
SPREAD_AT = SECOND_AT + 13
COPIES = SPREAD_AT + 7 + 3


def wrap(value, size):
    return lax.rem(value + size, size)


def kernel(
    widths_hbm,
    top_hbm,
    cot_hbm,
    first_hbm,
    second_hbm,
    rows_hbm,
    proj_hbm,
    ids_hbm,
    lens_hbm,
    out_first,
    out_second,
    out_pooled,
    top,
    cot,
    first,
    second,
    rows,
    proj,
    ids,
    lens,
    widths,
    hidden,
    slope,
    d_hidden,
    d_hidden_b,
    d_in,
    part,
    y_in,
    z_in,
    result,
    part2_b,
    y_own2,
    y_in2,
    z_in2,
    final2,
    result2,
    spread,
    passing,
    arrived,
    local_sem,
    send_sem,
    recv_sem,
):
    table = lax.axis_index("table")
    replica = lax.axis_index("replica")
    x = lax.div(table, 8)
    z = lax.rem(lax.div(table, 2), 4)
    c = lax.rem(table, 2)
    y = lax.div(replica, 4)
    zh = lax.rem(replica, 4)

    run = z * 2 + c

    def block(z_, c_, chunk=None):
        at = pl.ds(pl.multiple_of((z_ * 2 + c_) * BLOCK, BLOCK), BLOCK)
        if chunk is None:
            return cot.at[at]
        return cot.at[at, pl.ds(chunk * CHUNK, CHUNK)]

    def unit(x_):
        return pl.ds(pl.multiple_of(x_ * HIDDEN, HIDDEN), HIDDEN)

    def remote(number, src, dst, to_table, to_replica):
        return pltpu.make_async_remote_copy(
            src_ref=src,
            dst_ref=dst,
            send_sem=send_sem.at[number],
            recv_sem=recv_sem.at[number],
            device_id=(to_table, to_replica),
            device_id_type=MESH,
        )

    sent = []

    def send(number, src, dst, to_table, to_replica):
        copy = remote(number, src, dst, to_table, to_replica)
        copy.start()
        sent.append(copy)

    def receive(number, dst):
        remote(number, dst, dst, table, replica).wait_recv()

    def local(number, src, dst):
        copy = pltpu.make_async_copy(src, dst, local_sem.at[number])
        copy.start()
        return copy

    mine = block(z, c)
    load_cot = local(0, cot_hbm, mine)

    barrier = pltpu.get_barrier_semaphore()

    def greet(to_table, to_replica):
        pl.semaphore_signal(
            barrier, inc=1, device_id=(to_table, to_replica), device_id_type=MESH
        )

    for k in range(1, 8):
        greet(x * 8 + wrap(run + k, 8), replica)
    for k in range(1, 4):
        greet(wrap(x + k, 4) * 8 + run, replica)
    for k in range(1, 4):
        greet(table, wrap(y + k, 4) * 4 + zh)
    pairs = (y * 4 + zh + 1 - 2 * lax.rem(zh, 2), y * 4 + 3 - zh)
    greet(table, pairs[0])
    greet(table, pairs[1])
    load_first = local(1, first_hbm, first)
    load_top = local(2, top_hbm, top)
    load_ids = local(3, ids_hbm, ids)
    load_lens = local(4, lens_hbm, lens)
    load_rows = local(5, rows_hbm, rows)
    load_proj = local(6, proj_hbm, proj)
    run_at = pl.ds(pl.multiple_of(x * RUN, RUN), RUN)
    load_second = local(7, second_hbm.at[:, run_at], second.at[unit(x)])
    load_widths = local(8, widths_hbm, widths)
    load_cot.wait()
    pl.semaphore_wait(barrier, 15)

    run_z = (z, z + 1 - 2 * lax.rem(z, 2), wrap(z + 2, 4), 3 - z)
    def to_x(number, src, dst, k):
        send(number + k - 1, src, dst, wrap(x + k, 4) * 8 + run, replica)

    for r in range(CHUNKS):
        for v in (1, 3, 2):
            ref = block(z, c, r)
            send(Z_AT + 3 * r + v - 1, ref, ref, x * 8 + run_z[v] * 2 + c, replica)
    partner = x * 8 + z * 2 + 1 - c
    send(CORE_AT, mine, mine, partner, replica)

    for k in (1, 3, 2):
        to = pl.ds(pl.multiple_of(wrap(x + k, 4) * RUN, RUN), RUN)
        to_x(WEIGHT_AT, second_hbm.at[:, to], second.at[unit(x)], k)

    load_first.wait()
    load_top.wait()

    def forward(step, carry):
        at = pl.ds(pl.multiple_of(step * 256, 256), 256)
        pre = lax.dot_general(
            first[...], top[at, :], (((1,), (1,)), ((), ())), preferred_element_type=F32
        )
        s = 1.0 / (1.0 + jnp.exp(-pre))
        hidden[unit(x), at] = (pre * s).astype(BF16)
        slope[:, at] = s * (1.0 + pre * (1.0 - s))
        return carry

    lax.fori_loop(0, 4, forward, 0)
    for k in (1, 3, 2):
        to_x(HIDDEN_AT, hidden.at[unit(x)], hidden.at[unit(x)], k)

    load_ids.wait()
    load_lens.wait()
    load_rows.wait()
    load_proj.wait()
    load_widths.wait()

    def pool(t):
        slots = lax.broadcasted_iota(jnp.int32, (16, LANES), 0)
        live = jnp.where(slots < lens[t : t + 1, :], ids[t], -1)
        numbers = lax.broadcasted_iota(jnp.int32, (LANES, LANES), 0)
        counts = jnp.zeros((LANES, LANES), F32)
        for k in range(16):
            counts = counts + jnp.where(live[k : k + 1, :] == numbers, 1.0, 0.0)
        counts = counts.T.astype(BF16)
        whole = rows[t]
        high = whole.astype(BF16)
        rest = whole - high.astype(F32)
        middle = rest.astype(BF16)
        low = (rest - middle.astype(F32)).astype(BF16)
        pooled = jnp.dot(counts, low, preferred_element_type=F32)
        pooled = pooled + jnp.dot(counts, middle, preferred_element_type=F32)
        pooled = pooled + jnp.dot(counts, high, preferred_element_type=F32)
        lanes = lax.broadcasted_iota(jnp.int32, (LANES, LANES), 1)
        kept = jnp.where(lanes < widths[t], pooled, 0.0).astype(BF16)
        return jnp.dot(kept, proj[t], preferred_element_type=F32)

    def pool_pair(t):
        upper = pool(t).reshape(PEERS, 8, LANES)
        lower = pool(t + 2).reshape(PEERS, 8, LANES)
        both = jnp.concatenate([upper, lower], 1).astype(BF16)
        for to in range(4):
            spread[:, to, :, t * LANES : (t + 1) * LANES] = both[to * 8 : (to + 1) * 8]

    def share(y_):
        return pl.ds(pl.multiple_of(y_ * SHARE, SHARE), SHARE)

    def gather(r):
        for v in (1, 3, 2):
            ref = block(run_z[v], c, r)
            receive(Z_AT + 3 * r + v - 1, ref)
            send(CORE_AT + 1 + 3 * r + v - 1, ref, ref, partner, replica)

    def products(r):
        if r == 0:
            load_second.wait()
            for k in range(1, 4):
                receive(WEIGHT_AT + k - 1, second.at[unit(wrap(x - k, 4))])
            receive(CORE_AT, block(z, 1 - c))
        for v in (1, 3, 2):
            receive(CORE_AT + 1 + 3 * r + v - 1, block(run_z[v], 1 - c, r))
        at = slice(r * CHUNK, (r + 1) * CHUNK)
        value = jnp.dot(second[...], cot[:, at], preferred_element_type=F32)
        d_hidden[:, at] = value
        d_hidden_b[:, at] = value.astype(BF16)
        at = pl.ds(r * CHUNK, CHUNK)
        for k in (2, 1, 3):
            to_x(
                PARTIAL_AT + 3 * r,
                d_hidden_b.at[unit(wrap(x + k, 4)), at],
                d_in.at[k - 1, :, at],
                k,
            )

    def d_pre(r):
        at = pl.ds(r * CHUNK, CHUNK)
        total = d_hidden[unit(x), at]
        for k in (1, 3, 2):
            receive(PARTIAL_AT + 3 * r + k - 1, d_in.at[k - 1, :, at])
        for k in range(1, 4):
            total = total + d_in[k - 1, :, at].astype(F32)
        return (total * slope[:, at]).astype(BF16)

    def first_chunk(r):
        value = jnp.dot(d_pre(r), top[r * CHUNK : (r + 1) * CHUNK], preferred_element_type=F32)
        if r == 0:
            part[...] = value
        else:
            part[...] += value

    def first_last():
        r = CHUNKS - 1
        left = d_pre(r)
        for p in range(PIECES):
            at = slice(p * PIECE, (p + 1) * PIECE)
            value = part[:, at] + jnp.dot(
                left, top[r * CHUNK :, at], preferred_element_type=F32
            )
            part[:, at] = value
            at = pl.ds(p * PIECE, PIECE)
            for k in (2, 1, 3):
                to = wrap(y + k, 4)
                send(
                    FIRST_AT + 8 * p + k - 1,
                    part.at[share(to), at],
                    y_in.at[k - 1, :, at],
                    table,
                    to * 4 + zh,
                )

    def exchange(p):
        at = pl.ds(p * PIECE, PIECE)
        total = part[share(y), at]
        for k in (1, 3, 2):
            receive(FIRST_AT + 8 * p + k - 1, y_in.at[k - 1, :, at])
        for k in range(1, 4):
            total = total + y_in[k - 1, :, at]
        z_in[p, 0] = total.astype(BF16)
        send(FIRST_AT + 8 * p + 3, z_in.at[p, 0], z_in.at[p, 1], table, pairs[p % 2])

    def pair(p):
        receive(FIRST_AT + 8 * p + 3, z_in.at[p, 1])
        z_in[p, 2] = (z_in[p, 0].astype(F32) + z_in[p, 1].astype(F32)).astype(BF16)
        send(FIRST_AT + 8 * p + 4, z_in.at[p, 2], z_in.at[p, 3], table, pairs[1 - p % 2])

    def finish(p):
        receive(FIRST_AT + 8 * p + 4, z_in.at[p, 3])
        at = pl.ds(p * PIECE, PIECE)
        result[share(y), at] = (z_in[p, 2].astype(F32) + z_in[p, 3].astype(F32)).astype(BF16)
        ref = result.at[share(y), at]
        for k in (2, 1, 3):
            send(FIRST_AT + 8 * p + 5 + k - 1, ref, ref, table, wrap(y + k, 4) * 4 + zh)

    def collect(p):
        for k in (1, 3, 2):
            ref = result.at[share(wrap(y - k, 4)), pl.ds(p * PIECE, PIECE)]
            receive(FIRST_AT + 8 * p + 5 + k - 1, ref)

    def second_out():
        for k in range(1, 4):
            receive(HIDDEN_AT + k - 1, hidden.at[unit(wrap(x - k, 4))])
        value = lax.dot_general(
            hidden[...], cot[...], (((1,), (1,)), ((), ())), preferred_element_type=F32
        )
        y_own2[...] = value
        part2_b[...] = value.astype(BF16)
        for k in (2, 1, 3):
            to = wrap(y + k, 4)
            send(SECOND_AT + k - 1, part2_b.at[unit(to)], y_in2.at[k - 1], table, to * 4 + zh)

    def second_exchange():
        for k in (1, 3, 2):
            receive(SECOND_AT + k - 1, y_in2.at[k - 1])
        total = y_own2[unit(y), :]
        for k in range(1, 4):
            total = total + y_in2[k - 1].astype(F32)
        for h in range(2):
            z_in2[h, 0] = total[:, h * 256 : (h + 1) * 256].astype(BF16)
            send(SECOND_AT + 3 + h, z_in2.at[h, 0], z_in2.at[h, 1], table, pairs[h])

    def second_pair():
        for h in range(2):
            receive(SECOND_AT + 3 + h, z_in2.at[h, 1])
            z_in2[h, 2] = (z_in2[h, 0].astype(F32) + z_in2[h, 1].astype(F32)).astype(BF16)
            send(SECOND_AT + 5 + h, z_in2.at[h, 2], z_in2.at[h, 3], table, pairs[1 - h])

    def second_finish():
        for h in range(2):
            receive(SECOND_AT + 5 + h, z_in2.at[h, 3])
            final2[unit(y), h * 256 : (h + 1) * 256] = (
                z_in2[h, 2].astype(F32) + z_in2[h, 3].astype(F32)
            ).astype(BF16)
        ref = final2.at[unit(y)]
        for k in (2, 1, 3):
            send(SECOND_AT + 7 + k - 1, ref, ref, table, wrap(y + k, 4) * 4 + zh)

    def second_turn():
        for k in (1, 3, 2):
            receive(SECOND_AT + 7 + k - 1, final2.at[unit(wrap(y - k, 4))])
        for k in (2, 1, 3):
            to_x(SECOND_AT + 10, final2.at[unit(wrap(x + k, 4))], result2.at[:, run_at], k)
        result2[:, run_at] = final2[unit(x), :]

    def second_collect():
        for k in (1, 3, 2):
            at = pl.ds(pl.multiple_of(wrap(x - k, 4) * RUN, RUN), RUN)
            receive(SECOND_AT + 10 + k - 1, result2.at[:, at])

    def spread_run():
        for k in range(1, 8):
            to = wrap(run + k, 8)
            send(SPREAD_AT + k - 1, spread.at[to], passing.at[:, run], x * 8 + to, replica)
        passing[:, run] = spread[run]

    def spread_x():
        for k in range(1, 8):
            receive(SPREAD_AT + k - 1, passing.at[:, wrap(run - k, 8)])
        for k in (1, 3, 2):
            to = wrap(x + k, 4)
            send(SPREAD_AT + 7 + k - 1, passing.at[to], arrived.at[x], to * 8 + run, replica)
        arrived[x] = passing[x]

    def place_pooled():
        for k in (1, 3, 2):
            receive(SPREAD_AT + 7 + k - 1, arrived.at[wrap(x - k, 4)])

        def place(j, carry):
            value = arrived[lax.div(j, 8), lax.rem(j, 8)].astype(F32)
            start = pl.multiple_of(j * 1024, 1024)
            out_pooled[0, :, pl.ds(start, 512)] = value[:8].astype(BF16)
            out_pooled[0, :, pl.ds(start + 512, 512)] = value[8:].astype(BF16)
            return carry

        lax.fori_loop(0, PEERS, place, 0)

    pool_pair(0)
    gather(0)
    pool_pair(1)
    gather(1)
    products(0)
    gather(2)
    products(1)
    first_chunk(0)
    gather(3)
    spread_run()
    products(2)
    first_chunk(1)
    products(3)
    second_out()
    first_chunk(2)
    first_last()
    second_exchange()
    spread_x()
    for p in range(PIECES):
        exchange(p)
    second_pair()
    for p in range(PIECES):
        pair(p)
    second_finish()
    for copy in sent:
        copy.wait_send()
    sent.clear()
    place_pooled()
    for p in range(PIECES):
        finish(p)
    second_turn()
    for p in range(PIECES):
        collect(p)
    second_collect()
    out_first[...] = result[...]
    out_second[...] = result2[...]
    for copy in sent:
        copy.wait_send()


def shards(
    top_input,
    cotangent,
    w_first,
    w_second,
    sectioned_rows,
    projection,
    bag_ids,
    bag_lengths,
    table_width,
):
    hbm = pl.BlockSpec(memory_space=pltpu.HBM)
    vmem = pl.BlockSpec(memory_space=pltpu.VMEM)
    ids = jnp.transpose(bag_ids[0], (1, 2, 0))
    lens = jnp.transpose(bag_lengths[0], (1, 0))
    return pl.pallas_call(
        kernel,
        out_shape=(
            jax.ShapeDtypeStruct((HIDDEN, FEATS), BF16),
            jax.ShapeDtypeStruct((HIDDEN, FEATS), BF16),
            jax.ShapeDtypeStruct((1, 8, PEERS * 1024), BF16),
        ),
        in_specs=[hbm] * 9,
        out_specs=(vmem, vmem, vmem),
        scratch_shapes=[
            pltpu.VMEM((ROWS, FEATS), BF16),
            pltpu.VMEM((RUN, ROWS), BF16),
            pltpu.VMEM((HIDDEN, FEATS), BF16),
            pltpu.VMEM((LINE, RUN), BF16),
            pltpu.VMEM((TABLES, LANES, LANES), F32),
            pltpu.VMEM((TABLES, LANES, LANES), BF16),
            pltpu.VMEM((TABLES, 16, LANES), jnp.int32),
            pltpu.VMEM((TABLES, LANES), jnp.int32),
            pltpu.SMEM((TABLES,), jnp.int32),
            pltpu.VMEM((LINE, ROWS), BF16),
            pltpu.VMEM((HIDDEN, ROWS), F32),
            pltpu.VMEM((LINE, ROWS), F32),
            pltpu.VMEM((LINE, ROWS), BF16),
            pltpu.VMEM((3, HIDDEN, ROWS), BF16),
            pltpu.VMEM((HIDDEN, FEATS), F32),
            pltpu.VMEM((3, SHARE, FEATS), F32),
            pltpu.VMEM((PIECES, 4, SHARE, PIECE), BF16),
            pltpu.VMEM((HIDDEN, FEATS), BF16),
            pltpu.VMEM((LINE, RUN), BF16),
            pltpu.VMEM((LINE, RUN), F32),
            pltpu.VMEM((3, HIDDEN, RUN), BF16),
            pltpu.VMEM((2, 4, HIDDEN, RUN // 2), BF16),
            pltpu.VMEM((LINE, RUN), BF16),
            pltpu.VMEM((HIDDEN, FEATS), BF16),
            pltpu.VMEM((8, 4, 16, 512), BF16),
            pltpu.VMEM((4, 8, 16, 512), BF16),
            pltpu.VMEM((4, 8, 16, 512), BF16),
            pltpu.SemaphoreType.DMA((9,)),
            pltpu.SemaphoreType.DMA((COPIES,)),
            pltpu.SemaphoreType.DMA((COPIES,)),
        ],
        compiler_params=pltpu.CompilerParams(
            collective_id=0, has_side_effects=True, vmem_limit_bytes=40 * 2**20
        ),
        cost_estimate=pl.CostEstimate(
            flops=2 * 4 * HIDDEN * ROWS * FEATS, bytes_accessed=8 * 2**20, transcendentals=HIDDEN * ROWS
        ),
    )(
        *(
            pltpu.with_memory_space_constraint(value, pltpu.HBM)
            for value in (
                table_width,
                top_input,
                cotangent,
                w_first,
                w_second,
                sectioned_rows[0],
                projection,
                ids,
                lens,
            )
        )
    )


def solution(mesh):
    placed = (
        P("replica", None),
        P("table", "replica"),
        P("table", None),
        P("table", None),
        P("replica", "table", None, None),
        P("table", None, None),
        P("replica", None, "table", None),
        P("replica", None, "table"),
        P("table"),
    )
    return jax.shard_map(
        shards,
        mesh=mesh,
        in_specs=placed,
        out_specs=(P("table", None), P("table", None), P("replica", "table", None)),
        check_vma=False,
    )
```

```python
import jax
import jax.numpy as jnp
from jax import lax
from jax.experimental import pallas as pl
from jax.experimental.pallas import tpu as pltpu
from jax.sharding import PartitionSpec as P

MESH = pl.DeviceIdType.MESH
F32 = jnp.float32
BF16 = jnp.bfloat16

HIDDEN = 64
ROWS = 1024
FEATS = 2048
BLOCK = 64
RUN = 512
HALF = RUN // 2
LINE = 256
CHUNKS = 4
CHUNK = ROWS // CHUNKS
PIECES = 2
PIECE = FEATS // PIECES
SHARE = 16
PEERS = 32
TABLES = 4
LANES = 256

Z_AT = 0
CORE_AT = Z_AT + 3 * CHUNKS
PARTIAL_AT = CORE_AT + 1 + 3 * CHUNKS
WEIGHT_AT = PARTIAL_AT + 3 * CHUNKS
HIDDEN_AT = WEIGHT_AT + 3
FIRST_AT = HIDDEN_AT + 3
SECOND_AT = FIRST_AT + 8 * PIECES
SPREAD_AT = SECOND_AT + 11 * 2
COPIES = SPREAD_AT + 7 + 3


def wrap(value, size):
    return lax.rem(value + size, size)


def kernel(
    widths_hbm,
    top_hbm,
    cot_hbm,
    first_hbm,
    second_hbm,
    rows_hbm,
    proj_hbm,
    ids_hbm,
    lens_hbm,
    out_first,
    out_second,
    out_pooled,
    top,
    cot,
    first,
    second,
    rows,
    proj,
    ids,
    lens,
    widths,
    hidden,
    slope,
    d_hidden,
    d_hidden_b,
    d_in,
    part,
    part_b,
    y_in,
    z_in,
    result,
    part2_b,
    y_own2,
    y_in2,
    z_in2,
    final2,
    result2,
    spread,
    passing,
    arrived,
    local_sem,
    send_sem,
    recv_sem,
):
    table = lax.axis_index("table")
    replica = lax.axis_index("replica")
    x = lax.div(table, 8)
    z = lax.rem(lax.div(table, 2), 4)
    c = lax.rem(table, 2)
    y = lax.div(replica, 4)
    zh = lax.rem(replica, 4)

    run = z * 2 + c

    def block(z_, c_, chunk=None):
        at = pl.ds(pl.multiple_of((z_ * 2 + c_) * BLOCK, BLOCK), BLOCK)
        if chunk is None:
            return cot.at[at]
        return cot.at[at, pl.ds(chunk * CHUNK, CHUNK)]

    def unit(x_):
        return pl.ds(pl.multiple_of(x_ * HIDDEN, HIDDEN), HIDDEN)

    def remote(number, src, dst, to_table, to_replica):
        return pltpu.make_async_remote_copy(
            src_ref=src,
            dst_ref=dst,
            send_sem=send_sem.at[number],
            recv_sem=recv_sem.at[number],
            device_id=(to_table, to_replica),
            device_id_type=MESH,
        )

    sent = []

    def send(number, src, dst, to_table, to_replica):
        copy = remote(number, src, dst, to_table, to_replica)
        copy.start()
        sent.append(copy)

    def receive(number, dst):
        remote(number, dst, dst, table, replica).wait_recv()

    def local(number, src, dst):
        copy = pltpu.make_async_copy(src, dst, local_sem.at[number])
        copy.start()
        return copy

    mine = block(z, c)
    load_cot = local(0, cot_hbm, mine)

    barrier = pltpu.get_barrier_semaphore()

    def greet(to_table, to_replica):
        pl.semaphore_signal(
            barrier, inc=1, device_id=(to_table, to_replica), device_id_type=MESH
        )

    for k in range(1, 8):
        greet(x * 8 + wrap(run + k, 8), replica)
    for k in range(1, 4):
        greet(wrap(x + k, 4) * 8 + run, replica)
    for k in range(1, 4):
        greet(table, wrap(y + k, 4) * 4 + zh)
    pairs = (y * 4 + zh + 1 - 2 * lax.rem(zh, 2), y * 4 + 3 - zh)
    greet(table, pairs[0])
    greet(table, pairs[1])

    load_first = local(1, first_hbm, first)
    load_top = local(2, top_hbm, top)
    load_ids = local(3, ids_hbm, ids)
    load_lens = local(4, lens_hbm, lens)
    load_rows = local(5, rows_hbm, rows)
    load_proj = local(6, proj_hbm, proj)
    run_at = pl.ds(pl.multiple_of(x * RUN, RUN), RUN)
    load_second = local(7, second_hbm.at[:, run_at], second.at[unit(x)])
    load_widths = local(8, widths_hbm, widths)
    load_cot.wait()
    pl.semaphore_wait(barrier, 15)

    run_z = (z, z + 1 - 2 * lax.rem(z, 2), wrap(z + 2, 4), 3 - z)
    def to_x(number, src, dst, k):
        send(number + k - 1, src, dst, wrap(x + k, 4) * 8 + run, replica)

    for r in range(CHUNKS):
        for v in (1, 3, 2):
            ref = block(z, c, r)
            send(Z_AT + 3 * r + v - 1, ref, ref, x * 8 + run_z[v] * 2 + c, replica)
    partner = x * 8 + z * 2 + 1 - c
    send(CORE_AT, mine, mine, partner, replica)

    for k in (1, 3, 2):
        to = pl.ds(pl.multiple_of(wrap(x + k, 4) * RUN, RUN), RUN)
        to_x(WEIGHT_AT, second_hbm.at[:, to], second.at[unit(x)], k)

    load_first.wait()
    load_top.wait()

    def forward(step, carry):
        at = pl.ds(pl.multiple_of(step * 256, 256), 256)
        pre = lax.dot_general(
            first[...], top[at, :], (((1,), (1,)), ((), ())), preferred_element_type=F32
        )
        s = 1.0 / (1.0 + jnp.exp(-pre))
        hidden[unit(x), at] = (pre * s).astype(BF16)
        slope[:, at] = s * (1.0 + pre * (1.0 - s))
        return carry

    lax.fori_loop(0, 4, forward, 0)
    for k in (1, 3, 2):
        to_x(HIDDEN_AT, hidden.at[unit(x)], hidden.at[unit(x)], k)

    load_ids.wait()
    load_lens.wait()
    load_rows.wait()
    load_proj.wait()
    load_widths.wait()

    def pool(t):
        slots = lax.broadcasted_iota(jnp.int32, (16, LANES), 0)
        live = jnp.where(slots < lens[t : t + 1, :], ids[t], -1)
        numbers = lax.broadcasted_iota(jnp.int32, (LANES, LANES), 0)
        counts = jnp.zeros((LANES, LANES), F32)
        for k in range(16):
            counts = counts + jnp.where(live[k : k + 1, :] == numbers, 1.0, 0.0)
        counts = counts.T.astype(BF16)
        whole = rows[t]
        high = whole.astype(BF16)
        rest = whole - high.astype(F32)
        middle = rest.astype(BF16)
        low = (rest - middle.astype(F32)).astype(BF16)
        pooled = jnp.dot(counts, low, preferred_element_type=F32)
        pooled = pooled + jnp.dot(counts, middle, preferred_element_type=F32)
        pooled = pooled + jnp.dot(counts, high, preferred_element_type=F32)
        lanes = lax.broadcasted_iota(jnp.int32, (LANES, LANES), 1)
        kept = jnp.where(lanes < widths[t], pooled, 0.0).astype(BF16)
        return jnp.dot(kept, proj[t], preferred_element_type=F32)

    def pool_pair(t):
        upper = pool(t).reshape(PEERS, 8, LANES)
        lower = pool(t + 2).reshape(PEERS, 8, LANES)
        both = jnp.concatenate([upper, lower], 1).astype(BF16)
        for to in range(4):
            spread[:, to, :, t * LANES : (t + 1) * LANES] = both[to * 8 : (to + 1) * 8]

    def share(y_):
        return pl.ds(pl.multiple_of(y_ * SHARE, SHARE), SHARE)

    def gather(r):
        for v in (1, 3, 2):
            ref = block(run_z[v], c, r)
            receive(Z_AT + 3 * r + v - 1, ref)
            send(CORE_AT + 1 + 3 * r + v - 1, ref, ref, partner, replica)

    def products(r):
        if r == 0:
            load_second.wait()
            for k in range(1, 4):
                receive(WEIGHT_AT + k - 1, second.at[unit(wrap(x - k, 4))])
            receive(CORE_AT, block(z, 1 - c))
        for v in (1, 3, 2):
            receive(CORE_AT + 1 + 3 * r + v - 1, block(run_z[v], 1 - c, r))
        at = slice(r * CHUNK, (r + 1) * CHUNK)
        value = jnp.dot(second[...], cot[:, at], preferred_element_type=F32)
        d_hidden[:, at] = value
        d_hidden_b[:, at] = value.astype(BF16)
        at = pl.ds(r * CHUNK, CHUNK)
        for k in (2, 1, 3):
            to_x(
                PARTIAL_AT + 3 * r,
                d_hidden_b.at[unit(wrap(x + k, 4)), at],
                d_in.at[k - 1, :, at],
                k,
            )

    def d_pre(r):
        at = pl.ds(r * CHUNK, CHUNK)
        total = d_hidden[unit(x), at]
        for k in (1, 3, 2):
            receive(PARTIAL_AT + 3 * r + k - 1, d_in.at[k - 1, :, at])
        for k in range(1, 4):
            total = total + d_in[k - 1, :, at].astype(F32)
        return (total * slope[:, at]).astype(BF16)

    def first_chunk(r):
        value = jnp.dot(d_pre(r), top[r * CHUNK : (r + 1) * CHUNK], preferred_element_type=F32)
        if r == 0:
            part[...] = value
        else:
            part[...] += value

    def first_last():
        r = CHUNKS - 1
        left = d_pre(r)
        for p in range(PIECES):
            at = slice(p * PIECE, (p + 1) * PIECE)
            value = part[:, at] + jnp.dot(
                left, top[r * CHUNK :, at], preferred_element_type=F32
            )
            part[:, at] = value
            part_b[:, at] = value.astype(BF16)
            at = pl.ds(p * PIECE, PIECE)
            for k in (2, 1, 3):
                to = wrap(y + k, 4)
                send(
                    FIRST_AT + 8 * p + k - 1,
                    part_b.at[share(to), at],
                    y_in.at[k - 1, :, at],
                    table,
                    to * 4 + zh,
                )

    def exchange(p):
        at = pl.ds(p * PIECE, PIECE)
        total = part[share(y), at]
        for k in (1, 3, 2):
            receive(FIRST_AT + 8 * p + k - 1, y_in.at[k - 1, :, at])
        for k in range(1, 4):
            total = total + y_in[k - 1, :, at].astype(F32)
        z_in[p, 0] = total.astype(BF16)
        send(FIRST_AT + 8 * p + 3, z_in.at[p, 0], z_in.at[p, 1], table, pairs[p % 2])

    def pair(p):
        receive(FIRST_AT + 8 * p + 3, z_in.at[p, 1])
        z_in[p, 2] = (z_in[p, 0].astype(F32) + z_in[p, 1].astype(F32)).astype(BF16)
        send(FIRST_AT + 8 * p + 4, z_in.at[p, 2], z_in.at[p, 3], table, pairs[1 - p % 2])

    def finish(p):
        receive(FIRST_AT + 8 * p + 4, z_in.at[p, 3])
        at = pl.ds(p * PIECE, PIECE)
        result[share(y), at] = (z_in[p, 2].astype(F32) + z_in[p, 3].astype(F32)).astype(BF16)
        ref = result.at[share(y), at]
        for k in (2, 1, 3):
            send(FIRST_AT + 8 * p + 5 + k - 1, ref, ref, table, wrap(y + k, 4) * 4 + zh)

    def collect(p):
        for k in (1, 3, 2):
            ref = result.at[share(wrap(y - k, 4)), pl.ds(p * PIECE, PIECE)]
            receive(FIRST_AT + 8 * p + 5 + k - 1, ref)

    def second_out():
        for k in range(1, 4):
            receive(HIDDEN_AT + k - 1, hidden.at[unit(wrap(x - k, 4))])
        value = lax.dot_general(
            hidden[...], cot[...], (((1,), (1,)), ((), ())), preferred_element_type=F32
        )
        y_own2[...] = value
        part2_b[...] = value.astype(BF16)
        for h in range(2):
            at = pl.ds(h * HALF, HALF)
            for k in (2, 1, 3):
                to = wrap(y + k, 4)
                send(
                    SECOND_AT + 11 * h + k - 1,
                    part2_b.at[unit(to), at],
                    y_in2.at[k - 1, :, at],
                    table,
                    to * 4 + zh,
                )

    def second_exchange(h):
        at = pl.ds(h * HALF, HALF)
        total = y_own2[unit(y), at]
        for k in (1, 3, 2):
            receive(SECOND_AT + 11 * h + k - 1, y_in2.at[k - 1, :, at])
        for k in range(1, 4):
            total = total + y_in2[k - 1, :, at].astype(F32)
        z_in2[h, 0] = total.astype(BF16)
        send(SECOND_AT + 11 * h + 3, z_in2.at[h, 0], z_in2.at[h, 1], table, pairs[h])

    def second_pair(h):
        receive(SECOND_AT + 11 * h + 3, z_in2.at[h, 1])
        z_in2[h, 2] = (z_in2[h, 0].astype(F32) + z_in2[h, 1].astype(F32)).astype(BF16)
        send(SECOND_AT + 11 * h + 4, z_in2.at[h, 2], z_in2.at[h, 3], table, pairs[1 - h])

    def second_finish(h):
        receive(SECOND_AT + 11 * h + 4, z_in2.at[h, 3])
        at = pl.ds(h * HALF, HALF)
        final2[unit(y), at] = (z_in2[h, 2].astype(F32) + z_in2[h, 3].astype(F32)).astype(BF16)
        ref = final2.at[unit(y), at]
        for k in (2, 1, 3):
            send(SECOND_AT + 11 * h + 5 + k - 1, ref, ref, table, wrap(y + k, 4) * 4 + zh)

    def second_at(x_, h):
        return pl.ds(pl.multiple_of(x_ * RUN + h * HALF, HALF), HALF)

    def second_turn(h):
        at = pl.ds(h * HALF, HALF)
        for k in (1, 3, 2):
            receive(SECOND_AT + 11 * h + 5 + k - 1, final2.at[unit(wrap(y - k, 4)), at])
        for k in (2, 1, 3):
            to_x(
                SECOND_AT + 11 * h + 8,
                final2.at[unit(wrap(x + k, 4)), at],
                result2.at[:, second_at(x, h)],
                k,
            )
        result2[:, second_at(x, h)] = final2[unit(x), at]

    def second_collect(h):
        for k in (1, 3, 2):
            receive(SECOND_AT + 11 * h + 8 + k - 1, result2.at[:, second_at(wrap(x - k, 4), h)])

    def spread_run():
        for k in range(1, 8):
            to = wrap(run + k, 8)
            send(SPREAD_AT + k - 1, spread.at[to], passing.at[:, run], x * 8 + to, replica)
        passing[:, run] = spread[run]

    def spread_x():
        for k in range(1, 8):
            receive(SPREAD_AT + k - 1, passing.at[:, wrap(run - k, 8)])
        for k in (1, 3, 2):
            to = wrap(x + k, 4)
            send(SPREAD_AT + 7 + k - 1, passing.at[to], arrived.at[x], to * 8 + run, replica)
        arrived[x] = passing[x]

    def place_pooled():
        for k in (1, 3, 2):
            receive(SPREAD_AT + 7 + k - 1, arrived.at[wrap(x - k, 4)])

        def place(j, carry):
            value = arrived[lax.div(j, 8), lax.rem(j, 8)].astype(F32)
            start = pl.multiple_of(j * 1024, 1024)
            out_pooled[0, :, pl.ds(start, 512)] = value[:8].astype(BF16)
            out_pooled[0, :, pl.ds(start + 512, 512)] = value[8:].astype(BF16)
            return carry

        lax.fori_loop(0, PEERS, place, 0)

    pool_pair(0)
    pool_pair(1)
    for r in range(CHUNKS):
        gather(r)
    spread_run()
    for r in range(CHUNKS):
        products(r)
    second_out()
    for r in range(CHUNKS - 1):
        first_chunk(r)
    first_last()
    second_exchange(0)
    second_exchange(1)
    spread_x()
    for p in range(PIECES):
        exchange(p)
    second_pair(0)
    second_pair(1)
    for p in range(PIECES):
        pair(p)
    second_finish(0)
    second_finish(1)
    for copy in sent:
        copy.wait_send()
    sent.clear()
    place_pooled()
    second_turn(0)
    for p in range(PIECES):
        finish(p)
    second_turn(1)
    for p in range(PIECES):
        collect(p)
    second_collect(0)
    second_collect(1)
    out_first[...] = result[...]
    out_second[...] = result2[...]
    for copy in sent:
        copy.wait_send()


def shards(
    top_input,
    cotangent,
    w_first,
    w_second,
    sectioned_rows,
    projection,
    bag_ids,
    bag_lengths,
    table_width,
):
    hbm = pl.BlockSpec(memory_space=pltpu.HBM)
    vmem = pl.BlockSpec(memory_space=pltpu.VMEM)
    ids = jnp.transpose(bag_ids[0], (1, 2, 0))
    lens = jnp.transpose(bag_lengths[0], (1, 0))
    return pl.pallas_call(
        kernel,
        out_shape=(
            jax.ShapeDtypeStruct((HIDDEN, FEATS), BF16),
            jax.ShapeDtypeStruct((HIDDEN, FEATS), BF16),
            jax.ShapeDtypeStruct((1, 8, PEERS * 1024), BF16),
        ),
        in_specs=[hbm] * 9,
        out_specs=(vmem, vmem, vmem),
        scratch_shapes=[
            pltpu.VMEM((ROWS, FEATS), BF16),
            pltpu.VMEM((RUN, ROWS), BF16),
            pltpu.VMEM((HIDDEN, FEATS), BF16),
            pltpu.VMEM((LINE, RUN), BF16),
            pltpu.VMEM((TABLES, LANES, LANES), F32),
            pltpu.VMEM((TABLES, LANES, LANES), BF16),
            pltpu.VMEM((TABLES, 16, LANES), jnp.int32),
            pltpu.VMEM((TABLES, LANES), jnp.int32),
            pltpu.SMEM((TABLES,), jnp.int32),
            pltpu.VMEM((LINE, ROWS), BF16),
            pltpu.VMEM((HIDDEN, ROWS), F32),
            pltpu.VMEM((LINE, ROWS), F32),
            pltpu.VMEM((LINE, ROWS), BF16),
            pltpu.VMEM((3, HIDDEN, ROWS), BF16),
            pltpu.VMEM((HIDDEN, FEATS), F32),
            pltpu.VMEM((HIDDEN, FEATS), BF16),
            pltpu.VMEM((3, SHARE, FEATS), BF16),
            pltpu.VMEM((PIECES, 4, SHARE, PIECE), BF16),
            pltpu.VMEM((HIDDEN, FEATS), BF16),
            pltpu.VMEM((LINE, RUN), BF16),
            pltpu.VMEM((LINE, RUN), F32),
            pltpu.VMEM((3, HIDDEN, RUN), BF16),
            pltpu.VMEM((2, 4, HIDDEN, RUN // 2), BF16),
            pltpu.VMEM((LINE, RUN), BF16),
            pltpu.VMEM((HIDDEN, FEATS), BF16),
            pltpu.VMEM((8, 4, 16, 512), BF16),
            pltpu.VMEM((4, 8, 16, 512), BF16),
            pltpu.VMEM((4, 8, 16, 512), BF16),
            pltpu.SemaphoreType.DMA((9,)),
            pltpu.SemaphoreType.DMA((COPIES,)),
            pltpu.SemaphoreType.DMA((COPIES,)),
        ],
        compiler_params=pltpu.CompilerParams(
            collective_id=0, has_side_effects=True, vmem_limit_bytes=40 * 2**20
        ),
        cost_estimate=pl.CostEstimate(
            flops=2 * 4 * HIDDEN * ROWS * FEATS, bytes_accessed=8 * 2**20, transcendentals=HIDDEN * ROWS
        ),
    )(
        *(
            pltpu.with_memory_space_constraint(value, pltpu.HBM)
            for value in (
                table_width,
                top_input,
                cotangent,
                w_first,
                w_second,
                sectioned_rows[0],
                projection,
                ids,
                lens,
            )
        )
    )


def solution(mesh):
    placed = (
        P("replica", None),
        P("table", "replica"),
        P("table", None),
        P("table", None),
        P("replica", "table", None, None),
        P("table", None, None),
        P("replica", None, "table", None),
        P("replica", None, "table"),
        P("table"),
    )
    return jax.shard_map(
        shards,
        mesh=mesh,
        in_specs=placed,
        out_specs=(P("table", None), P("table", None), P("replica", "table", None)),
        check_vma=False,
    )
```

```python
import jax
import jax.numpy as jnp
from jax import lax
from jax.experimental import pallas as pl
from jax.experimental.pallas import tpu as pltpu
from jax.sharding import PartitionSpec as P

MESH = pl.DeviceIdType.MESH
F32 = jnp.float32
BF16 = jnp.bfloat16

HIDDEN = 64
ROWS = 1024
FEATS = 2048
BLOCK = 64
RUN = 512
SLICES = 4
SLICE = RUN // SLICES
LINE = 256
CHUNKS = 4
CHUNK = ROWS // CHUNKS
PIECES = 2
PIECE = FEATS // PIECES
SHARE = 16
PEERS = 32
TABLES = 4
LANES = 256

Z_AT = 0
CORE_AT = Z_AT + 3 * CHUNKS
PARTIAL_AT = CORE_AT + 1 + 3 * CHUNKS
WEIGHT_AT = PARTIAL_AT + 3 * CHUNKS
HIDDEN_AT = WEIGHT_AT + 3
FIRST_AT = HIDDEN_AT + 3
SECOND_AT = FIRST_AT + 8 * PIECES
SPREAD_AT = SECOND_AT + 11 * SLICES
COPIES = SPREAD_AT + 7 + 3


def wrap(value, size):
    return lax.rem(value + size, size)


def kernel(
    widths_hbm,
    top_hbm,
    cot_hbm,
    first_hbm,
    second_hbm,
    rows_hbm,
    proj_hbm,
    ids_hbm,
    lens_hbm,
    out_first,
    out_second,
    out_pooled,
    top,
    cot,
    first,
    second,
    rows,
    proj,
    ids,
    lens,
    widths,
    hidden,
    slope,
    d_hidden,
    d_hidden_b,
    d_in,
    part,
    part_b,
    y_in,
    z_in,
    result,
    part2_b,
    y_own2,
    y_in2,
    z_in2,
    final2,
    result2,
    spread,
    passing,
    arrived,
    local_sem,
    send_sem,
    recv_sem,
):
    table = lax.axis_index("table")
    replica = lax.axis_index("replica")
    x = lax.div(table, 8)
    z = lax.rem(lax.div(table, 2), 4)
    c = lax.rem(table, 2)
    y = lax.div(replica, 4)
    zh = lax.rem(replica, 4)

    run = z * 2 + c

    def block(z_, c_, chunk=None):
        at = pl.ds(pl.multiple_of((z_ * 2 + c_) * BLOCK, BLOCK), BLOCK)
        if chunk is None:
            return cot.at[at]
        return cot.at[at, pl.ds(chunk * CHUNK, CHUNK)]

    def unit(x_):
        return pl.ds(pl.multiple_of(x_ * HIDDEN, HIDDEN), HIDDEN)

    def remote(number, src, dst, to_table, to_replica):
        return pltpu.make_async_remote_copy(
            src_ref=src,
            dst_ref=dst,
            send_sem=send_sem.at[number],
            recv_sem=recv_sem.at[number],
            device_id=(to_table, to_replica),
            device_id_type=MESH,
        )

    sent = []

    def send(number, src, dst, to_table, to_replica):
        copy = remote(number, src, dst, to_table, to_replica)
        copy.start()
        sent.append(copy)

    def receive(number, dst):
        remote(number, dst, dst, table, replica).wait_recv()

    def local(number, src, dst):
        copy = pltpu.make_async_copy(src, dst, local_sem.at[number])
        copy.start()
        return copy

    mine = block(z, c)
    load_cot = local(0, cot_hbm, mine)

    barrier = pltpu.get_barrier_semaphore()

    def greet(to_table, to_replica):
        pl.semaphore_signal(
            barrier, inc=1, device_id=(to_table, to_replica), device_id_type=MESH
        )

    for k in range(1, 8):
        greet(x * 8 + wrap(run + k, 8), replica)
    for k in range(1, 4):
        greet(wrap(x + k, 4) * 8 + run, replica)
    for k in range(1, 4):
        greet(table, wrap(y + k, 4) * 4 + zh)
    pairs = (y * 4 + zh + 1 - 2 * lax.rem(zh, 2), y * 4 + 3 - zh)
    greet(table, pairs[0])
    greet(table, pairs[1])

    load_first = local(1, first_hbm, first)
    load_top = local(2, top_hbm, top)
    load_ids = local(3, ids_hbm, ids)
    load_lens = local(4, lens_hbm, lens)
    load_rows = local(5, rows_hbm, rows)
    load_proj = local(6, proj_hbm, proj)
    run_at = pl.ds(pl.multiple_of(x * RUN, RUN), RUN)
    load_second = local(7, second_hbm.at[:, run_at], second.at[unit(x)])
    load_widths = local(8, widths_hbm, widths)
    load_cot.wait()
    pl.semaphore_wait(barrier, 15)

    run_z = (z, z + 1 - 2 * lax.rem(z, 2), wrap(z + 2, 4), 3 - z)
    def to_x(number, src, dst, k):
        send(number + k - 1, src, dst, wrap(x + k, 4) * 8 + run, replica)

    for r in range(CHUNKS):
        for v in (1, 3, 2):
            ref = block(z, c, r)
            send(Z_AT + 3 * r + v - 1, ref, ref, x * 8 + run_z[v] * 2 + c, replica)
    partner = x * 8 + z * 2 + 1 - c
    send(CORE_AT, mine, mine, partner, replica)

    for k in (1, 3, 2):
        to = pl.ds(pl.multiple_of(wrap(x + k, 4) * RUN, RUN), RUN)
        to_x(WEIGHT_AT, second_hbm.at[:, to], second.at[unit(x)], k)

    load_first.wait()
    load_top.wait()

    def forward(step, carry):
        at = pl.ds(pl.multiple_of(step * 256, 256), 256)
        pre = lax.dot_general(
            first[...], top[at, :], (((1,), (1,)), ((), ())), preferred_element_type=F32
        )
        s = 1.0 / (1.0 + jnp.exp(-pre))
        hidden[unit(x), at] = (pre * s).astype(BF16)
        slope[:, at] = s * (1.0 + pre * (1.0 - s))
        return carry

    lax.fori_loop(0, 4, forward, 0)
    for k in (1, 3, 2):
        to_x(HIDDEN_AT, hidden.at[unit(x)], hidden.at[unit(x)], k)

    load_ids.wait()
    load_lens.wait()
    load_rows.wait()
    load_proj.wait()
    load_widths.wait()

    def pool(t):
        slots = lax.broadcasted_iota(jnp.int32, (16, LANES), 0)
        live = jnp.where(slots < lens[t : t + 1, :], ids[t], -1)
        numbers = lax.broadcasted_iota(jnp.int32, (LANES, LANES), 0)
        counts = jnp.zeros((LANES, LANES), F32)
        for k in range(16):
            counts = counts + jnp.where(live[k : k + 1, :] == numbers, 1.0, 0.0)
        counts = counts.T.astype(BF16)
        whole = rows[t]
        high = whole.astype(BF16)
        rest = whole - high.astype(F32)
        middle = rest.astype(BF16)
        low = (rest - middle.astype(F32)).astype(BF16)
        pooled = jnp.dot(counts, low, preferred_element_type=F32)
        pooled = pooled + jnp.dot(counts, middle, preferred_element_type=F32)
        pooled = pooled + jnp.dot(counts, high, preferred_element_type=F32)
        lanes = lax.broadcasted_iota(jnp.int32, (LANES, LANES), 1)
        kept = jnp.where(lanes < widths[t], pooled, 0.0).astype(BF16)
        return jnp.dot(kept, proj[t], preferred_element_type=F32)

    def pool_pair(t):
        upper = pool(t).reshape(PEERS, 8, LANES)
        lower = pool(t + 2).reshape(PEERS, 8, LANES)
        both = jnp.concatenate([upper, lower], 1).astype(BF16)
        for to in range(4):
            spread[:, to, :, t * LANES : (t + 1) * LANES] = both[to * 8 : (to + 1) * 8]

    def share(y_):
        return pl.ds(pl.multiple_of(y_ * SHARE, SHARE), SHARE)

    def gather(r):
        for v in (1, 3, 2):
            ref = block(run_z[v], c, r)
            receive(Z_AT + 3 * r + v - 1, ref)
            send(CORE_AT + 1 + 3 * r + v - 1, ref, ref, partner, replica)

    def products(r):
        if r == 0:
            load_second.wait()
            for k in range(1, 4):
                receive(WEIGHT_AT + k - 1, second.at[unit(wrap(x - k, 4))])
            receive(CORE_AT, block(z, 1 - c))
        for v in (1, 3, 2):
            receive(CORE_AT + 1 + 3 * r + v - 1, block(run_z[v], 1 - c, r))
        at = slice(r * CHUNK, (r + 1) * CHUNK)
        value = jnp.dot(second[...], cot[:, at], preferred_element_type=F32)
        d_hidden[:, at] = value
        d_hidden_b[:, at] = value.astype(BF16)
        at = pl.ds(r * CHUNK, CHUNK)
        for k in (2, 1, 3):
            to_x(
                PARTIAL_AT + 3 * r,
                d_hidden_b.at[unit(wrap(x + k, 4)), at],
                d_in.at[k - 1, :, at],
                k,
            )

    def d_pre(r):
        at = pl.ds(r * CHUNK, CHUNK)
        total = d_hidden[unit(x), at]
        for k in (1, 3, 2):
            receive(PARTIAL_AT + 3 * r + k - 1, d_in.at[k - 1, :, at])
        for k in range(1, 4):
            total = total + d_in[k - 1, :, at].astype(F32)
        return (total * slope[:, at]).astype(BF16)

    def first_chunk(r):
        value = jnp.dot(d_pre(r), top[r * CHUNK : (r + 1) * CHUNK], preferred_element_type=F32)
        if r == 0:
            part[...] = value
        else:
            part[...] += value

    def first_last():
        r = CHUNKS - 1
        left = d_pre(r)
        for p in range(PIECES):
            at = slice(p * PIECE, (p + 1) * PIECE)
            value = part[:, at] + jnp.dot(
                left, top[r * CHUNK :, at], preferred_element_type=F32
            )
            part[:, at] = value
            part_b[:, at] = value.astype(BF16)
            at = pl.ds(p * PIECE, PIECE)
            for k in (2, 1, 3):
                to = wrap(y + k, 4)
                send(
                    FIRST_AT + 8 * p + k - 1,
                    part_b.at[share(to), at],
                    y_in.at[k - 1, :, at],
                    table,
                    to * 4 + zh,
                )

    def exchange(p):
        at = pl.ds(p * PIECE, PIECE)
        total = part[share(y), at]
        for k in (1, 3, 2):
            receive(FIRST_AT + 8 * p + k - 1, y_in.at[k - 1, :, at])
        for k in range(1, 4):
            total = total + y_in[k - 1, :, at].astype(F32)
        z_in[p, 0] = total.astype(BF16)
        send(FIRST_AT + 8 * p + 3, z_in.at[p, 0], z_in.at[p, 1], table, pairs[p % 2])

    def pair(p):
        receive(FIRST_AT + 8 * p + 3, z_in.at[p, 1])
        z_in[p, 2] = (z_in[p, 0].astype(F32) + z_in[p, 1].astype(F32)).astype(BF16)
        send(FIRST_AT + 8 * p + 4, z_in.at[p, 2], z_in.at[p, 3], table, pairs[1 - p % 2])

    def finish(p):
        receive(FIRST_AT + 8 * p + 4, z_in.at[p, 3])
        at = pl.ds(p * PIECE, PIECE)
        result[share(y), at] = (z_in[p, 2].astype(F32) + z_in[p, 3].astype(F32)).astype(BF16)
        ref = result.at[share(y), at]
        for k in (2, 1, 3):
            send(FIRST_AT + 8 * p + 5 + k - 1, ref, ref, table, wrap(y + k, 4) * 4 + zh)

    def collect(p):
        for k in (1, 3, 2):
            ref = result.at[share(wrap(y - k, 4)), pl.ds(p * PIECE, PIECE)]
            receive(FIRST_AT + 8 * p + 5 + k - 1, ref)

    def second_out():
        for k in range(1, 4):
            receive(HIDDEN_AT + k - 1, hidden.at[unit(wrap(x - k, 4))])
        value = lax.dot_general(
            hidden[...], cot[...], (((1,), (1,)), ((), ())), preferred_element_type=F32
        )
        y_own2[...] = value
        part2_b[...] = value.astype(BF16)
        for h in range(SLICES):
            at = pl.ds(h * SLICE, SLICE)
            for k in (2, 1, 3):
                to = wrap(y + k, 4)
                send(
                    SECOND_AT + 11 * h + k - 1,
                    part2_b.at[unit(to), at],
                    y_in2.at[k - 1, :, at],
                    table,
                    to * 4 + zh,
                )

    def second_exchange(h):
        at = pl.ds(h * SLICE, SLICE)
        total = y_own2[unit(y), at]
        for k in (1, 3, 2):
            receive(SECOND_AT + 11 * h + k - 1, y_in2.at[k - 1, :, at])
        for k in range(1, 4):
            total = total + y_in2[k - 1, :, at].astype(F32)
        z_in2[h, 0] = total.astype(BF16)
        send(SECOND_AT + 11 * h + 3, z_in2.at[h, 0], z_in2.at[h, 1], table, pairs[h % 2])

    def second_pair(h):
        receive(SECOND_AT + 11 * h + 3, z_in2.at[h, 1])
        z_in2[h, 2] = (z_in2[h, 0].astype(F32) + z_in2[h, 1].astype(F32)).astype(BF16)
        send(SECOND_AT + 11 * h + 4, z_in2.at[h, 2], z_in2.at[h, 3], table, pairs[1 - h % 2])

    def second_finish(h):
        receive(SECOND_AT + 11 * h + 4, z_in2.at[h, 3])
        at = pl.ds(h * SLICE, SLICE)
        final2[unit(y), at] = (z_in2[h, 2].astype(F32) + z_in2[h, 3].astype(F32)).astype(BF16)
        ref = final2.at[unit(y), at]
        for k in (2, 1, 3):
            send(SECOND_AT + 11 * h + 5 + k - 1, ref, ref, table, wrap(y + k, 4) * 4 + zh)

    def second_at(x_, h):
        return pl.ds(pl.multiple_of(x_ * RUN + h * SLICE, SLICE), SLICE)

    def second_turn(h):
        at = pl.ds(h * SLICE, SLICE)
        for k in (1, 3, 2):
            receive(SECOND_AT + 11 * h + 5 + k - 1, final2.at[unit(wrap(y - k, 4)), at])
        for k in (2, 1, 3):
            to_x(
                SECOND_AT + 11 * h + 8,
                final2.at[unit(wrap(x + k, 4)), at],
                result2.at[:, second_at(x, h)],
                k,
            )
        result2[:, second_at(x, h)] = final2[unit(x), at]

    def second_collect(h):
        for k in (1, 3, 2):
            receive(SECOND_AT + 11 * h + 8 + k - 1, result2.at[:, second_at(wrap(x - k, 4), h)])

    def spread_run():
        for k in range(1, 8):
            to = wrap(run + k, 8)
            send(SPREAD_AT + k - 1, spread.at[to], passing.at[:, run], x * 8 + to, replica)
        passing[:, run] = spread[run]

    def spread_x():
        for k in range(1, 8):
            receive(SPREAD_AT + k - 1, passing.at[:, wrap(run - k, 8)])
        for k in (1, 3, 2):
            to = wrap(x + k, 4)
            send(SPREAD_AT + 7 + k - 1, passing.at[to], arrived.at[x], to * 8 + run, replica)
        arrived[x] = passing[x]

    def place_pooled():
        for k in (1, 3, 2):
            receive(SPREAD_AT + 7 + k - 1, arrived.at[wrap(x - k, 4)])

        def place(j, carry):
            value = arrived[lax.div(j, 8), lax.rem(j, 8)].astype(F32)
            start = pl.multiple_of(j * 1024, 1024)
            out_pooled[0, :, pl.ds(start, 512)] = value[:8].astype(BF16)
            out_pooled[0, :, pl.ds(start + 512, 512)] = value[8:].astype(BF16)
            return carry

        lax.fori_loop(0, PEERS, place, 0)

    pool_pair(0)
    pool_pair(1)
    for r in range(CHUNKS):
        gather(r)
    spread_run()
    for r in range(CHUNKS):
        products(r)
    second_out()
    for r in range(CHUNKS - 1):
        first_chunk(r)
    first_last()
    for h in range(SLICES):
        second_exchange(h)
    spread_x()
    for p in range(PIECES):
        exchange(p)
    for h in range(SLICES):
        second_pair(h)
    for p in range(PIECES):
        pair(p)
    for h in range(SLICES):
        second_finish(h)
    for copy in sent:
        copy.wait_send()
    sent.clear()
    place_pooled()
    second_turn(0)
    for p in range(PIECES):
        finish(p)
    second_turn(1)
    second_turn(2)
    second_turn(3)
    for p in range(PIECES):
        collect(p)
    for h in range(SLICES):
        second_collect(h)
    out_first[...] = result[...]
    out_second[...] = result2[...]
    for copy in sent:
        copy.wait_send()


def shards(
    top_input,
    cotangent,
    w_first,
    w_second,
    sectioned_rows,
    projection,
    bag_ids,
    bag_lengths,
    table_width,
):
    hbm = pl.BlockSpec(memory_space=pltpu.HBM)
    vmem = pl.BlockSpec(memory_space=pltpu.VMEM)
    ids = jnp.transpose(bag_ids[0], (1, 2, 0))
    lens = jnp.transpose(bag_lengths[0], (1, 0))
    return pl.pallas_call(
        kernel,
        out_shape=(
            jax.ShapeDtypeStruct((HIDDEN, FEATS), BF16),
            jax.ShapeDtypeStruct((HIDDEN, FEATS), BF16),
            jax.ShapeDtypeStruct((1, 8, PEERS * 1024), BF16),
        ),
        in_specs=[hbm] * 9,
        out_specs=(vmem, vmem, vmem),
        scratch_shapes=[
            pltpu.VMEM((ROWS, FEATS), BF16),
            pltpu.VMEM((RUN, ROWS), BF16),
            pltpu.VMEM((HIDDEN, FEATS), BF16),
            pltpu.VMEM((LINE, RUN), BF16),
            pltpu.VMEM((TABLES, LANES, LANES), F32),
            pltpu.VMEM((TABLES, LANES, LANES), BF16),
            pltpu.VMEM((TABLES, 16, LANES), jnp.int32),
            pltpu.VMEM((TABLES, LANES), jnp.int32),
            pltpu.SMEM((TABLES,), jnp.int32),
            pltpu.VMEM((LINE, ROWS), BF16),
            pltpu.VMEM((HIDDEN, ROWS), F32),
            pltpu.VMEM((LINE, ROWS), F32),
            pltpu.VMEM((LINE, ROWS), BF16),
            pltpu.VMEM((3, HIDDEN, ROWS), BF16),
            pltpu.VMEM((HIDDEN, FEATS), F32),
            pltpu.VMEM((HIDDEN, FEATS), BF16),
            pltpu.VMEM((3, SHARE, FEATS), BF16),
            pltpu.VMEM((PIECES, 4, SHARE, PIECE), BF16),
            pltpu.VMEM((HIDDEN, FEATS), BF16),
            pltpu.VMEM((LINE, RUN), BF16),
            pltpu.VMEM((LINE, RUN), F32),
            pltpu.VMEM((3, HIDDEN, RUN), BF16),
            pltpu.VMEM((4, 4, HIDDEN, SLICE), BF16),
            pltpu.VMEM((LINE, RUN), BF16),
            pltpu.VMEM((HIDDEN, FEATS), BF16),
            pltpu.VMEM((8, 4, 16, 512), BF16),
            pltpu.VMEM((4, 8, 16, 512), BF16),
            pltpu.VMEM((4, 8, 16, 512), BF16),
            pltpu.SemaphoreType.DMA((9,)),
            pltpu.SemaphoreType.DMA((COPIES,)),
            pltpu.SemaphoreType.DMA((COPIES,)),
        ],
        compiler_params=pltpu.CompilerParams(
            collective_id=0, has_side_effects=True, vmem_limit_bytes=40 * 2**20
        ),
        cost_estimate=pl.CostEstimate(
            flops=2 * 4 * HIDDEN * ROWS * FEATS, bytes_accessed=8 * 2**20, transcendentals=HIDDEN * ROWS
        ),
    )(
        *(
            pltpu.with_memory_space_constraint(value, pltpu.HBM)
            for value in (
                table_width,
                top_input,
                cotangent,
                w_first,
                w_second,
                sectioned_rows[0],
                projection,
                ids,
                lens,
            )
        )
    )


def solution(mesh):
    placed = (
        P("replica", None),
        P("table", "replica"),
        P("table", None),
        P("table", None),
        P("replica", "table", None, None),
        P("table", None, None),
        P("replica", None, "table", None),
        P("replica", None, "table"),
        P("table"),
    )
    return jax.shard_map(
        shards,
        mesh=mesh,
        in_specs=placed,
        out_specs=(P("table", None), P("table", None), P("replica", "table", None)),
        check_vma=False,
    )
```

```python
import jax
import jax.numpy as jnp
from jax import lax
from jax.experimental import pallas as pl
from jax.experimental.pallas import tpu as pltpu
from jax.sharding import PartitionSpec as P

MESH = pl.DeviceIdType.MESH
F32 = jnp.float32
BF16 = jnp.bfloat16

HIDDEN = 64
ROWS = 1024
FEATS = 2048
BLOCK = 64
RUN = 512
SLICES = 4
SLICE = RUN // SLICES
LINE = 256
CHUNKS = 4
CHUNK = ROWS // CHUNKS
PIECES = 2
PIECE = FEATS // PIECES
SHARE = 16
PEERS = 32
TABLES = 4
LANES = 256

Z_AT = 0
CORE_AT = Z_AT + 3 * CHUNKS
PARTIAL_AT = CORE_AT + 1 + 3 * CHUNKS
WEIGHT_AT = PARTIAL_AT + 3 * CHUNKS
HIDDEN_AT = WEIGHT_AT + 3
FIRST_AT = HIDDEN_AT + 3
SECOND_AT = FIRST_AT + 8 * PIECES
SPREAD_AT = SECOND_AT + 11 * SLICES
COPIES = SPREAD_AT + 7 + 3


def wrap(value, size):
    return lax.rem(value + size, size)


def kernel(
    widths_hbm,
    top_hbm,
    cot_hbm,
    first_hbm,
    second_hbm,
    rows_hbm,
    proj_hbm,
    ids_hbm,
    lens_hbm,
    out_first,
    out_second,
    out_pooled,
    top,
    cot,
    first,
    second,
    rows,
    proj,
    ids,
    lens,
    widths,
    hidden,
    slope,
    d_hidden,
    d_hidden_b,
    d_in,
    part,
    part_b,
    y_in,
    z_in,
    result,
    part2_b,
    y_own2,
    y_in2,
    z_in2,
    final2,
    result2,
    spread,
    passing,
    arrived,
    local_sem,
    send_sem,
    recv_sem,
):
    table = lax.axis_index("table")
    replica = lax.axis_index("replica")
    x = lax.div(table, 8)
    z = lax.rem(lax.div(table, 2), 4)
    c = lax.rem(table, 2)
    y = lax.div(replica, 4)
    zh = lax.rem(replica, 4)

    run = z * 2 + c

    def block(z_, c_, chunk=None):
        at = pl.ds(pl.multiple_of((z_ * 2 + c_) * BLOCK, BLOCK), BLOCK)
        if chunk is None:
            return cot.at[at]
        return cot.at[at, pl.ds(chunk * CHUNK, CHUNK)]

    def unit(x_):
        return pl.ds(pl.multiple_of(x_ * HIDDEN, HIDDEN), HIDDEN)

    def remote(number, src, dst, to_table, to_replica):
        return pltpu.make_async_remote_copy(
            src_ref=src,
            dst_ref=dst,
            send_sem=send_sem.at[number],
            recv_sem=recv_sem.at[number],
            device_id=(to_table, to_replica),
            device_id_type=MESH,
        )

    sent = []

    def send(number, src, dst, to_table, to_replica):
        copy = remote(number, src, dst, to_table, to_replica)
        copy.start()
        sent.append(copy)

    def receive(number, dst):
        remote(number, dst, dst, table, replica).wait_recv()

    def local(number, src, dst):
        copy = pltpu.make_async_copy(src, dst, local_sem.at[number])
        copy.start()
        return copy

    mine = block(z, c)
    load_cot = local(0, cot_hbm, mine)

    barrier = pltpu.get_barrier_semaphore()

    def greet(to_table, to_replica):
        pl.semaphore_signal(
            barrier, inc=1, device_id=(to_table, to_replica), device_id_type=MESH
        )

    for k in range(1, 8):
        greet(x * 8 + wrap(run + k, 8), replica)
    for k in range(1, 4):
        greet(wrap(x + k, 4) * 8 + run, replica)
    for k in range(1, 4):
        greet(table, wrap(y + k, 4) * 4 + zh)
    pairs = (y * 4 + zh + 1 - 2 * lax.rem(zh, 2), y * 4 + 3 - zh)
    greet(table, pairs[0])
    greet(table, pairs[1])

    load_first = local(1, first_hbm, first)
    load_top = local(2, top_hbm, top)
    load_ids = local(3, ids_hbm, ids)
    load_lens = local(4, lens_hbm, lens)
    load_rows = local(5, rows_hbm, rows)
    load_proj = local(6, proj_hbm, proj)
    run_at = pl.ds(pl.multiple_of(x * RUN, RUN), RUN)
    load_second = local(7, second_hbm.at[:, run_at], second.at[unit(x)])
    load_widths = local(8, widths_hbm, widths)
    load_cot.wait()
    pl.semaphore_wait(barrier, 15)

    run_z = (z, z + 1 - 2 * lax.rem(z, 2), wrap(z + 2, 4), 3 - z)
    def to_x(number, src, dst, k):
        send(number + k - 1, src, dst, wrap(x + k, 4) * 8 + run, replica)

    for r in range(CHUNKS):
        for v in (1, 3, 2):
            ref = block(z, c, r)
            send(Z_AT + 3 * r + v - 1, ref, ref, x * 8 + run_z[v] * 2 + c, replica)
    partner = x * 8 + z * 2 + 1 - c
    send(CORE_AT, mine, mine, partner, replica)

    for k in (1, 3, 2):
        to = pl.ds(pl.multiple_of(wrap(x + k, 4) * RUN, RUN), RUN)
        to_x(WEIGHT_AT, second_hbm.at[:, to], second.at[unit(x)], k)

    load_first.wait()
    load_top.wait()

    def forward(step, carry):
        at = pl.ds(pl.multiple_of(step * 256, 256), 256)
        pre = lax.dot_general(
            first[...], top[at, :], (((1,), (1,)), ((), ())), preferred_element_type=F32
        )
        s = 1.0 / (1.0 + jnp.exp(-pre))
        hidden[unit(x), at] = (pre * s).astype(BF16)
        slope[:, at] = s * (1.0 + pre * (1.0 - s))
        return carry

    lax.fori_loop(0, 4, forward, 0)
    for k in (1, 3, 2):
        to_x(HIDDEN_AT, hidden.at[unit(x)], hidden.at[unit(x)], k)

    load_ids.wait()
    load_lens.wait()
    load_rows.wait()
    load_proj.wait()
    load_widths.wait()

    def pool(t):
        slots = lax.broadcasted_iota(jnp.int32, (16, LANES), 0)
        live = jnp.where(slots < lens[t : t + 1, :], ids[t], -1)
        numbers = lax.broadcasted_iota(jnp.int32, (LANES, LANES), 0)
        counts = jnp.zeros((LANES, LANES), F32)
        for k in range(16):
            counts = counts + jnp.where(live[k : k + 1, :] == numbers, 1.0, 0.0)
        counts = counts.T.astype(BF16)
        whole = rows[t]
        high = whole.astype(BF16)
        rest = whole - high.astype(F32)
        middle = rest.astype(BF16)
        low = (rest - middle.astype(F32)).astype(BF16)
        pooled = jnp.dot(counts, low, preferred_element_type=F32)
        pooled = pooled + jnp.dot(counts, middle, preferred_element_type=F32)
        pooled = pooled + jnp.dot(counts, high, preferred_element_type=F32)
        lanes = lax.broadcasted_iota(jnp.int32, (LANES, LANES), 1)
        kept = jnp.where(lanes < widths[t], pooled, 0.0).astype(BF16)
        return jnp.dot(kept, proj[t], preferred_element_type=F32)

    def pool_pair(t):
        upper = pool(t).reshape(PEERS, 8, LANES)
        lower = pool(t + 2).reshape(PEERS, 8, LANES)
        both = jnp.concatenate([upper, lower], 1).astype(BF16)
        for to in range(4):
            spread[:, to, :, t * LANES : (t + 1) * LANES] = both[to * 8 : (to + 1) * 8]

    def share(y_):
        return pl.ds(pl.multiple_of(y_ * SHARE, SHARE), SHARE)

    def gather(r):
        for v in (1, 3, 2):
            ref = block(run_z[v], c, r)
            receive(Z_AT + 3 * r + v - 1, ref)
            send(CORE_AT + 1 + 3 * r + v - 1, ref, ref, partner, replica)

    def products(r):
        if r == 0:
            load_second.wait()
            for k in range(1, 4):
                receive(WEIGHT_AT + k - 1, second.at[unit(wrap(x - k, 4))])
            receive(CORE_AT, block(z, 1 - c))
        for v in (1, 3, 2):
            receive(CORE_AT + 1 + 3 * r + v - 1, block(run_z[v], 1 - c, r))
        at = slice(r * CHUNK, (r + 1) * CHUNK)
        value = jnp.dot(second[...], cot[:, at], preferred_element_type=F32)
        d_hidden[:, at] = value
        d_hidden_b[:, at] = value.astype(BF16)
        at = pl.ds(r * CHUNK, CHUNK)
        for k in (1, 3, 2):
            to_x(
                PARTIAL_AT + 3 * r,
                d_hidden_b.at[unit(wrap(x + k, 4)), at],
                d_in.at[k - 1, :, at],
                k,
            )

    def d_pre(r):
        at = pl.ds(r * CHUNK, CHUNK)
        total = d_hidden[unit(x), at]
        for k in (1, 3, 2):
            receive(PARTIAL_AT + 3 * r + k - 1, d_in.at[k - 1, :, at])
        for k in range(1, 4):
            total = total + d_in[k - 1, :, at].astype(F32)
        return (total * slope[:, at]).astype(BF16)

    def first_chunk(r):
        value = jnp.dot(d_pre(r), top[r * CHUNK : (r + 1) * CHUNK], preferred_element_type=F32)
        if r == 0:
            part[...] = value
        else:
            part[...] += value

    def first_last():
        r = CHUNKS - 1
        left = d_pre(r)
        for p in range(PIECES):
            at = slice(p * PIECE, (p + 1) * PIECE)
            value = part[:, at] + jnp.dot(
                left, top[r * CHUNK :, at], preferred_element_type=F32
            )
            part[:, at] = value
            part_b[:, at] = value.astype(BF16)
            at = pl.ds(p * PIECE, PIECE)
            for k in (1, 3, 2):
                to = wrap(y + k, 4)
                send(
                    FIRST_AT + 8 * p + k - 1,
                    part_b.at[share(to), at],
                    y_in.at[k - 1, :, at],
                    table,
                    to * 4 + zh,
                )

    def exchange(p):
        at = pl.ds(p * PIECE, PIECE)
        total = part[share(y), at]
        for k in (1, 3, 2):
            receive(FIRST_AT + 8 * p + k - 1, y_in.at[k - 1, :, at])
        for k in range(1, 4):
            total = total + y_in[k - 1, :, at].astype(F32)
        z_in[p, 0] = total.astype(BF16)
        send(FIRST_AT + 8 * p + 3, z_in.at[p, 0], z_in.at[p, 1], table, pairs[p % 2])

    def pair(p):
        receive(FIRST_AT + 8 * p + 3, z_in.at[p, 1])
        z_in[p, 2] = (z_in[p, 0].astype(F32) + z_in[p, 1].astype(F32)).astype(BF16)
        send(FIRST_AT + 8 * p + 4, z_in.at[p, 2], z_in.at[p, 3], table, pairs[1 - p % 2])

    def finish(p):
        receive(FIRST_AT + 8 * p + 4, z_in.at[p, 3])
        at = pl.ds(p * PIECE, PIECE)
        result[share(y), at] = (z_in[p, 2].astype(F32) + z_in[p, 3].astype(F32)).astype(BF16)
        ref = result.at[share(y), at]
        for k in (1, 3, 2):
            send(FIRST_AT + 8 * p + 5 + k - 1, ref, ref, table, wrap(y + k, 4) * 4 + zh)

    def collect(p):
        for k in (1, 3, 2):
            ref = result.at[share(wrap(y - k, 4)), pl.ds(p * PIECE, PIECE)]
            receive(FIRST_AT + 8 * p + 5 + k - 1, ref)

    def second_out():
        for k in range(1, 4):
            receive(HIDDEN_AT + k - 1, hidden.at[unit(wrap(x - k, 4))])
        value = lax.dot_general(
            hidden[...], cot[...], (((1,), (1,)), ((), ())), preferred_element_type=F32
        )
        y_own2[...] = value
        part2_b[...] = value.astype(BF16)
        for h in range(SLICES):
            at = pl.ds(h * SLICE, SLICE)
            for k in (1, 3, 2):
                to = wrap(y + k, 4)
                send(
                    SECOND_AT + 11 * h + k - 1,
                    part2_b.at[unit(to), at],
                    y_in2.at[k - 1, :, at],
                    table,
                    to * 4 + zh,
                )

    def second_exchange(h):
        at = pl.ds(h * SLICE, SLICE)
        total = y_own2[unit(y), at]
        for k in (1, 3, 2):
            receive(SECOND_AT + 11 * h + k - 1, y_in2.at[k - 1, :, at])
        for k in range(1, 4):
            total = total + y_in2[k - 1, :, at].astype(F32)
        z_in2[h, 0] = total.astype(BF16)
        send(SECOND_AT + 11 * h + 3, z_in2.at[h, 0], z_in2.at[h, 1], table, pairs[h % 2])

    def second_pair(h):
        receive(SECOND_AT + 11 * h + 3, z_in2.at[h, 1])
        z_in2[h, 2] = (z_in2[h, 0].astype(F32) + z_in2[h, 1].astype(F32)).astype(BF16)
        send(SECOND_AT + 11 * h + 4, z_in2.at[h, 2], z_in2.at[h, 3], table, pairs[1 - h % 2])

    def second_finish(h):
        receive(SECOND_AT + 11 * h + 4, z_in2.at[h, 3])
        at = pl.ds(h * SLICE, SLICE)
        final2[unit(y), at] = (z_in2[h, 2].astype(F32) + z_in2[h, 3].astype(F32)).astype(BF16)
        ref = final2.at[unit(y), at]
        for k in (1, 3, 2):
            send(SECOND_AT + 11 * h + 5 + k - 1, ref, ref, table, wrap(y + k, 4) * 4 + zh)

    def second_at(x_, h):
        return pl.ds(pl.multiple_of(x_ * RUN + h * SLICE, SLICE), SLICE)

    def second_turn(h):
        at = pl.ds(h * SLICE, SLICE)
        for k in (1, 3, 2):
            receive(SECOND_AT + 11 * h + 5 + k - 1, final2.at[unit(wrap(y - k, 4)), at])
        for k in (1, 3, 2):
            to_x(
                SECOND_AT + 11 * h + 8,
                final2.at[unit(wrap(x + k, 4)), at],
                result2.at[:, second_at(x, h)],
                k,
            )
        result2[:, second_at(x, h)] = final2[unit(x), at]

    def second_collect(h):
        for k in (1, 3, 2):
            receive(SECOND_AT + 11 * h + 8 + k - 1, result2.at[:, second_at(wrap(x - k, 4), h)])

    def spread_run():
        for k in range(1, 8):
            to = wrap(run + k, 8)
            send(SPREAD_AT + k - 1, spread.at[to], passing.at[:, run], x * 8 + to, replica)
        passing[:, run] = spread[run]

    def spread_x():
        for k in range(1, 8):
            receive(SPREAD_AT + k - 1, passing.at[:, wrap(run - k, 8)])
        for k in (1, 3, 2):
            to = wrap(x + k, 4)
            send(SPREAD_AT + 7 + k - 1, passing.at[to], arrived.at[x], to * 8 + run, replica)
        arrived[x] = passing[x]

    def place_pooled():
        for k in (1, 3, 2):
            receive(SPREAD_AT + 7 + k - 1, arrived.at[wrap(x - k, 4)])

        def place(j, carry):
            value = arrived[lax.div(j, 8), lax.rem(j, 8)].astype(F32)
            start = pl.multiple_of(j * 1024, 1024)
            out_pooled[0, :, pl.ds(start, 512)] = value[:8].astype(BF16)
            out_pooled[0, :, pl.ds(start + 512, 512)] = value[8:].astype(BF16)
            return carry

        lax.fori_loop(0, PEERS, place, 0)

    pool_pair(0)
    pool_pair(1)
    for r in range(CHUNKS):
        gather(r)
    spread_run()
    for r in range(CHUNKS):
        products(r)
    second_out()
    for r in range(CHUNKS - 1):
        first_chunk(r)
    first_last()
    for h in range(SLICES):
        second_exchange(h)
    spread_x()
    for p in range(PIECES):
        exchange(p)
    for h in range(SLICES):
        second_pair(h)
    for p in range(PIECES):
        pair(p)
    for h in range(SLICES):
        second_finish(h)
    for copy in sent:
        copy.wait_send()
    sent.clear()
    place_pooled()
    second_turn(0)
    for p in range(PIECES):
        finish(p)
    second_turn(1)
    second_turn(2)
    second_turn(3)
    for p in range(PIECES):
        collect(p)
    for h in range(SLICES):
        second_collect(h)
    out_first[...] = result[...]
    out_second[...] = result2[...]
    for copy in sent:
        copy.wait_send()


def shards(
    top_input,
    cotangent,
    w_first,
    w_second,
    sectioned_rows,
    projection,
    bag_ids,
    bag_lengths,
    table_width,
):
    hbm = pl.BlockSpec(memory_space=pltpu.HBM)
    vmem = pl.BlockSpec(memory_space=pltpu.VMEM)
    ids = jnp.transpose(bag_ids[0], (1, 2, 0))
    lens = jnp.transpose(bag_lengths[0], (1, 0))
    return pl.pallas_call(
        kernel,
        out_shape=(
            jax.ShapeDtypeStruct((HIDDEN, FEATS), BF16),
            jax.ShapeDtypeStruct((HIDDEN, FEATS), BF16),
            jax.ShapeDtypeStruct((1, 8, PEERS * 1024), BF16),
        ),
        in_specs=[hbm] * 9,
        out_specs=(vmem, vmem, vmem),
        scratch_shapes=[
            pltpu.VMEM((ROWS, FEATS), BF16),
            pltpu.VMEM((RUN, ROWS), BF16),
            pltpu.VMEM((HIDDEN, FEATS), BF16),
            pltpu.VMEM((LINE, RUN), BF16),
            pltpu.VMEM((TABLES, LANES, LANES), F32),
            pltpu.VMEM((TABLES, LANES, LANES), BF16),
            pltpu.VMEM((TABLES, 16, LANES), jnp.int32),
            pltpu.VMEM((TABLES, LANES), jnp.int32),
            pltpu.SMEM((TABLES,), jnp.int32),
            pltpu.VMEM((LINE, ROWS), BF16),
            pltpu.VMEM((HIDDEN, ROWS), F32),
            pltpu.VMEM((LINE, ROWS), F32),
            pltpu.VMEM((LINE, ROWS), BF16),
            pltpu.VMEM((3, HIDDEN, ROWS), BF16),
            pltpu.VMEM((HIDDEN, FEATS), F32),
            pltpu.VMEM((HIDDEN, FEATS), BF16),
            pltpu.VMEM((3, SHARE, FEATS), BF16),
            pltpu.VMEM((PIECES, 4, SHARE, PIECE), BF16),
            pltpu.VMEM((HIDDEN, FEATS), BF16),
            pltpu.VMEM((LINE, RUN), BF16),
            pltpu.VMEM((LINE, RUN), F32),
            pltpu.VMEM((3, HIDDEN, RUN), BF16),
            pltpu.VMEM((4, 4, HIDDEN, SLICE), BF16),
            pltpu.VMEM((LINE, RUN), BF16),
            pltpu.VMEM((HIDDEN, FEATS), BF16),
            pltpu.VMEM((8, 4, 16, 512), BF16),
            pltpu.VMEM((4, 8, 16, 512), BF16),
            pltpu.VMEM((4, 8, 16, 512), BF16),
            pltpu.SemaphoreType.DMA((9,)),
            pltpu.SemaphoreType.DMA((COPIES,)),
            pltpu.SemaphoreType.DMA((COPIES,)),
        ],
        compiler_params=pltpu.CompilerParams(
            collective_id=0, has_side_effects=True, vmem_limit_bytes=40 * 2**20
        ),
        cost_estimate=pl.CostEstimate(
            flops=2 * 4 * HIDDEN * ROWS * FEATS, bytes_accessed=8 * 2**20, transcendentals=HIDDEN * ROWS
        ),
    )(
        *(
            pltpu.with_memory_space_constraint(value, pltpu.HBM)
            for value in (
                table_width,
                top_input,
                cotangent,
                w_first,
                w_second,
                sectioned_rows[0],
                projection,
                ids,
                lens,
            )
        )
    )


def solution(mesh):
    placed = (
        P("replica", None),
        P("table", "replica"),
        P("table", None),
        P("table", None),
        P("replica", "table", None, None),
        P("table", None, None),
        P("replica", None, "table", None),
        P("replica", None, "table"),
        P("table"),
    )
    return jax.shard_map(
        shards,
        mesh=mesh,
        in_specs=placed,
        out_specs=(P("table", None), P("table", None), P("replica", "table", None)),
        check_vma=False,
    )
```
